32 devices in a mesh: prow: 8 (over z, x), pcol: 4 (over y, core).
Axes of the slice: x: 2, y: 2, z: 4, core: 2. Of those that a mesh axis runs over, the one named last changes fastest.
Arguments:
- right_side: float32 [512, 8192], P('pcol', 'prow'), may hold values from -6 to 6
- factor: float32 [8192, 2048], P('prow', 'pcol'), may hold values from -0.125 to 0.125
- inverses: float32 [2048, 512], replicated, as said below
Outputs:
- solved: float32 [512, 8192], P('pcol', 'prow')
The draws below stay inside these ranges and needn't reach their ends.
Inputs may be any that keep to these rules, and one draw needn't show every extreme that they name: Each 512 x 512 block of inverses is lower triangular with a positive diagonal.
All inputs are finite; a program needn't handle non-finite values.
Results may differ from the reference program's by a relative error of at most 0.0001.
Values sent between devices are 32-bit elements; how exact they have to be, the bound alone decides.
A program may use at most 64 MiB of HBM per device.

```python
import jax
import jax.numpy as jnp
from jax import lax

NB = 512
STEPS = 4
NRHS = 512
RB_DEV = 2
M = 8192
N_PROW = 8


def draw_inverses(key, part):
    first_key, second_key = jax.random.split(jax.random.fold_in(key, 7))
    shape = (STEPS * NB, NB)
    offdiag = jax.random.normal(first_key, shape, jnp.float32) * (0.6 / NB ** 0.5)
    diagonal = jnp.exp(jax.random.uniform(second_key, (STEPS * NB, 1), jnp.float32, -0.6931472, 0.6931472))
    row_index = jnp.arange(STEPS * NB)[:, None] % NB
    col_index = jnp.arange(NB)[None, :]
    return jnp.where(row_index > col_index, offdiag, jnp.where(row_index == col_index, diagonal, 0.0)).astype(jnp.float32)


def shard_levels(rng, extent, cuts, smallest, largest):
    gain, own = 1.0, jax.random.fold_in(rng, 6)
    for dim, parts in cuts:
        heights = jnp.exp(jax.random.uniform(jax.random.fold_in(own, dim), (parts,), jnp.float32, smallest / len(cuts), largest / len(cuts)))
        gain = gain * jnp.repeat(heights, extent[dim] // parts).reshape([-1 if axis == dim else 1 for axis in range(len(extent))])
    return gain


def gaussian(key, shape, spread, most, cuts=(), dtype=jnp.bfloat16):
    loudness = shard_levels(key, shape, cuts, -0.22, 0.18) if cuts else 1.0
    values = jax.random.normal(key, shape, jnp.float32) * spread * loudness
    return jnp.minimum(jnp.maximum(values, -most), most).astype(dtype)


def setup_inputs(seed: int = 0) -> dict:
    key_list = jax.random.split(jax.random.key(seed), 4)
    return {
        "right_side": gaussian(key_list[0], (NRHS, M), 1.0, 6.0, ((0, 4), (1, 8)), jnp.float32),
        "factor": gaussian(key_list[1], (M, STEPS * NB), (STEPS * NB) ** -0.5, 0.125, ((0, 8), (1, 4)), jnp.float32),
        "inverses": draw_inverses(jax.random.fold_in(key_list[3], 71), 0),
    }


def contract(left, right):
    return lax.dot_general(left, right, (((1,), (1,)), ((), ())), precision=lax.Precision.HIGHEST, preferred_element_type=jnp.float32)


def reference(right_side, factor, inverses):
    total = NB * RB_DEV * N_PROW
    rhs_matrix = right_side.reshape(NRHS, N_PROW, RB_DEV, NB).transpose(0, 2, 1, 3).reshape(NRHS, total)
    lower = factor.reshape(N_PROW, RB_DEV, NB, STEPS * NB).transpose(1, 0, 2, 3).reshape(total, STEPS * NB)
    solved_list = []
    for section in range(STEPS):
        current = rhs_matrix[:, section * NB:(section + 1) * NB]
        for column in range(section):
            current = current - contract(solved_list[column], lower[section * NB:(section + 1) * NB, column * NB:(column + 1) * NB])
        solved_list.append(contract(current, inverses[section * NB:(section + 1) * NB]))
    trailing = rhs_matrix
    for column in range(STEPS):
        trailing = trailing - contract(solved_list[column], lower[:, column * NB:(column + 1) * NB])
    result = jnp.concatenate(solved_list + [trailing[:, STEPS * NB:]], axis=1)
    return result.reshape(NRHS, RB_DEV, N_PROW, NB).transpose(0, 2, 1, 3).reshape(NRHS, total)
```

```python
import functools

import jax
import jax.numpy as jnp
from jax import lax
from jax.experimental import pallas as pl
from jax.experimental.pallas import tpu as pltpu
from jax.sharding import PartitionSpec as P

MESH = pl.DeviceIdType.MESH
SUBS = 2
HALVES = 2


def split(value):
    high = value.astype(jnp.bfloat16)
    low = (value - high.astype(jnp.float32)).astype(jnp.bfloat16)
    return high, low


def dot_nt(left, right):
    return lax.dot_general(left, right, (((1,), (1,)), ((), ())), preferred_element_type=jnp.float32)


def contract(left, right_high, right_low):
    rows = left.shape[0]
    high, low = split(left)
    both = dot_nt(jnp.concatenate([high, low], axis=0), right_high)
    return both[:rows] + (both[rows:] + dot_nt(high, right_low))


def kernel(
    n_prow, sections, rhs, factor, inverses, out,
    fac, fac_hi, fac_lo, dinv, d_hi, d_lo, l_in, l_hi, l_lo,
    acc, x_own, x_head, x_all, part, pre, fin, cross,
    local_sem, l_send, l_fwd, l_recv, head_send, head_recv, gather_send,
    tree_send, x_recv, part_send, pre_recv, fin_recv, cross_recv,
):
    width = rhs.shape[0]
    block = factor.shape[1]
    blocks = factor.shape[0] // block
    p = lax.axis_index("prow")
    c = lax.axis_index("pcol")
    pair, parity = c // 2, c % 2
    mate = pair * 2 + 1 - parity
    over = (1 - pair) * 2 + parity
    far = (1 - pair) * 2 + 1 - parity
    in_head = p < sections
    sub = width // SUBS
    half = block // HALVES

    fac_copy = pltpu.make_async_copy(factor, fac, local_sem.at[0])
    fac_copy.start()
    dinv_copy = pltpu.make_async_copy(
        inverses.at[pl.ds(lax.rem(p, sections) * block, block)], dinv, local_sem.at[1]
    )
    dinv_copy.start()

    barrier = pltpu.get_barrier_semaphore()
    for step in range(1, n_prow):
        pl.semaphore_signal(
            barrier, inc=1, device_id=(lax.rem(p + step, n_prow), c), device_id_type=MESH
        )
    for step in range(1, sections):
        pl.semaphore_signal(
            barrier, inc=1, device_id=(p, lax.rem(c + step, sections)), device_id_type=MESH
        )
    pl.semaphore_wait(barrier, n_prow - 1 + sections - 1)

    def send(src, dst, send_sem, recv_sem, row, col):
        return pltpu.make_async_remote_copy(
            src_ref=src, dst_ref=dst, send_sem=send_sem, recv_sem=recv_sem,
            device_id=(row, col), device_id_type=MESH,
        )

    def l_piece(j, h):
        return l_in.at[j, pl.ds(h * half, half)]

    def l_copy(j, h, target, way):
        return send(
            factor.at[pl.ds(h * half, half)], l_piece(j, h), l_send.at[way, h], l_recv.at[j, h], p, target
        )

    def l_forward(j, h):
        return send(l_piece(j, h), l_piece(j, h), l_fwd.at[j, h], l_recv.at[j, h], p, j ^ 3)

    for j in range(sections - 1):
        @pl.when((p > j) & in_head & (c == j))
        def _():
            for h in range(HALVES):
                l_copy(j, h, j ^ 2, 0).start()
                l_copy(j, h, j ^ 1, 1).start()

    dinv_copy.wait()
    d_hi[...], d_lo[...] = split(dinv[...])
    fac_copy.wait()
    fac_hi[...], fac_lo[...] = split(fac[...])

    for j in range(sections - 1):
        @pl.when((p > j) & in_head & (c == j))
        def _():
            l_hi[j], l_lo[j] = fac_hi[:block], fac_lo[:block]

        @pl.when((p > j) & in_head & (c == (j ^ 2)))
        def _():
            for h in range(HALVES):
                l_forward(j, h).wait_recv()
                l_forward(j, h).start()
            l_hi[j], l_lo[j] = split(l_in[j])

    for j in range(sections - 1):
        @pl.when((p > j) & in_head & ((c == (j ^ 1)) | (c == (j ^ 3))))
        def _():
            for h in range(HALVES):
                l_forward(j, h).wait_recv()
            l_hi[j], l_lo[j] = split(l_in[j])

    def head_copy(s, target, col):
        rows = pl.ds(s * sub, sub)
        return send(
            x_own.at[rows], x_head.at[col, rows], head_send.at[target, s], head_recv.at[col, s], target, c
        )

    def gather_copy(s):
        rows = pl.ds(s * sub, sub)
        return send(x_own.at[rows], x_all.at[c, rows], gather_send.at[s], x_recv.at[c, s], p, p)

    @pl.when(in_head)
    def _():
        for s in range(SUBS):
            rows = pl.ds(s * sub, sub)
            acc[...] = rhs[rows, :block]
            for j in range(sections - 1):
                @pl.when(j < p)
                def _():
                    head_copy(s, sections - 1, j).wait_recv()
                    acc[...] -= contract(x_head[j, rows], l_hi[j], l_lo[j])
            x_own[rows] = contract(acc[...], d_hi[...], d_lo[...])
            for target in range(1, sections):
                @pl.when(p < target)
                def _():
                    head_copy(s, target, p).start()

            @pl.when(p != c)
            def _():
                gather_copy(s).start()

            @pl.when(p == c)
            def _():
                x_all[c, rows] = x_own[rows]

    z, x = p // 2, p % 2
    root_z, root_x = c // 2, c % 2
    links = (
        ((x == root_x) & (z >= root_z) & (z + 1 < n_prow // 2), p + 2),
        ((x == root_x) & (z <= root_z) & (z > 0), p - 2),
        (x == root_x, z * 2 + 1 - x),
    )

    def tree_copy(q, s, way, target):
        ref = x_all.at[q, pl.ds(s * sub, sub)]
        return send(ref, ref, tree_send.at[way, q, s], x_recv.at[q, s], target, c)

    def part_copy(i, r):
        if i == 0:
            return send(part.at[i, r], pre.at[r], part_send.at[i, r], pre_recv.at[r], p, mate)
        if i == 1:
            return send(part.at[i, r], cross.at[r], part_send.at[i, r], cross_recv.at[r], p, over)
        return send(part.at[i, r], fin.at[r], part_send.at[i, r], fin_recv.at[r], p, mate)

    def each_block(body):
        for r in range(blocks):
            if r == 0:
                pl.when(p >= sections)(functools.partial(body, r))
            else:
                body(r)

    order = (far, over, mate, c)
    for i, q in enumerate(order):
        for s in range(SUBS):
            @pl.when((p != c) | (q != c))
            def _():
                tree_copy(q, s, 2, mate).wait_recv()

            for way, (active, target) in enumerate(links):
                @pl.when(active)
                def _():
                    tree_copy(q, s, way, target).start()

        def update(r):
            cols = pl.ds(r * block, block)
            value = contract(x_all[q], fac_hi[cols], fac_lo[cols])
            if i == 1:
                part_copy(0, r).wait_recv()
                value = value + pre[r]
            part[i, r] = value
            if i < 3:
                part_copy(i, r).start()

        each_block(update)

    @pl.when(in_head)
    def _():
        out[:, :block] = x_own[...]

    def finish(r):
        cols = pl.ds(r * block, block)
        part_copy(2, r).wait_recv()
        part_copy(1, r).wait_recv()
        out[:, cols] = rhs[:, cols] - (part[3, r] + fin[r] + cross[r])
        for i in range(3):
            part_copy(i, r).wait_send()

    each_block(finish)

    for j in range(sections - 1):
        @pl.when((p > j) & in_head & (c == j))
        def _():
            for h in range(HALVES):
                l_copy(j, h, j ^ 2, 0).wait_send()
                l_copy(j, h, j ^ 1, 1).wait_send()

        @pl.when((p > j) & in_head & (c == (j ^ 2)))
        def _():
            for h in range(HALVES):
                l_forward(j, h).wait_send()

    @pl.when(in_head)
    def _():
        for s in range(SUBS):
            for target in range(1, sections):
                @pl.when(p < target)
                def _():
                    head_copy(s, target, p).wait_send()

            @pl.when(p != c)
            def _():
                gather_copy(s).wait_send()

    for q in order:
        for s in range(SUBS):
            for way, (active, target) in enumerate(links):
                @pl.when(active)
                def _():
                    tree_copy(q, s, way, target).wait_send()


def per_device(right_side, factor, inverses):
    width = right_side.shape[0]
    rows, block = factor.shape
    blocks = rows // block
    n_prow = lax.axis_size("prow")
    sections = lax.axis_size("pcol")
    f32, bf16 = jnp.float32, jnp.bfloat16
    vmem, dma = pltpu.VMEM, pltpu.SemaphoreType.DMA
    heads = sections - 1
    return pl.pallas_call(
        functools.partial(kernel, n_prow, sections),
        out_shape=jax.ShapeDtypeStruct(right_side.shape, f32),
        in_specs=[
            pl.BlockSpec(memory_space=pltpu.VMEM),
            pl.BlockSpec(memory_space=pl.ANY),
            pl.BlockSpec(memory_space=pl.ANY),
        ],
        out_specs=pl.BlockSpec(memory_space=pltpu.VMEM),
        scratch_shapes=[
            vmem((rows, block), f32), vmem((rows, block), bf16), vmem((rows, block), bf16),
            vmem((block, block), f32), vmem((block, block), bf16), vmem((block, block), bf16),
            vmem((heads, block, block), f32), vmem((heads, block, block), bf16), vmem((heads, block, block), bf16),
            vmem((width // SUBS, block), f32), vmem((width, block), f32),
            vmem((heads, width, block), f32), vmem((sections, width, block), f32),
            vmem((4, blocks, width, block), f32), vmem((blocks, width, block), f32),
            vmem((blocks, width, block), f32), vmem((blocks, width, block), f32),
            dma((2,)), dma((2, HALVES)), dma((heads, HALVES)), dma((heads, HALVES)),
            dma((sections, SUBS)), dma((heads, SUBS)), dma((SUBS,)),
            dma((3, sections, SUBS)), dma((sections, SUBS)), dma((3, blocks)),
            dma((blocks,)), dma((blocks,)), dma((blocks,)),
        ],
        compiler_params=pltpu.CompilerParams(
            collective_id=0, has_side_effects=True, vmem_limit_bytes=48 * 1024 * 1024
        ),
        name="solve_window",
    )(right_side, factor, inverses)


def solution(mesh):
    return jax.shard_map(
        per_device,
        mesh=mesh,
        in_specs=(P("pcol", "prow"), P("prow", "pcol"), P()),
        out_specs=P("pcol", "prow"),
        check_vma=False,
    )
```

```python
import functools

import jax
import jax.numpy as jnp
from jax import lax
from jax.experimental import pallas as pl
from jax.experimental.pallas import tpu as pltpu
from jax.sharding import PartitionSpec as P

MESH = pl.DeviceIdType.MESH
SUBS = 2
HALVES = 2
PIECES = 4


def split(value):
    high = value.astype(jnp.bfloat16)
    low = (value - high.astype(jnp.float32)).astype(jnp.bfloat16)
    return high, low


def dot_nt(left, right):
    return lax.dot_general(left, right, (((1,), (1,)), ((), ())), preferred_element_type=jnp.float32)


def contract(left, right_high, right_low):
    rows = left.shape[0]
    high, low = split(left)
    both = dot_nt(jnp.concatenate([high, low], axis=0), right_high)
    return both[:rows] + (both[rows:] + dot_nt(high, right_low))


def kernel(
    n_prow, sections, rhs, factor, inverses, out,
    fac, dinv, d_hi, d_lo, l_in, l_hi, l_lo, l_oth,
    acc, x_own, x_head, x_all, part, fin,
    local_sem, l_send, l_fwd, l_recv, swap_send, swap_recv, head_send, head_recv,
    source_send, tree_send, x_recv, part_send, fin_recv,
):
    width = rhs.shape[0]
    block = factor.shape[1]
    piece = factor.shape[0] // PIECES
    p = lax.axis_index("prow")
    c = lax.axis_index("pcol")
    pair, parity = c // 2, c % 2
    mate = pair * 2 + 1 - parity
    over = (1 - pair) * 2 + parity
    z, x = p // 2, p % 2
    beside = z * 2 + 1 - x
    levels = n_prow // 2
    in_head = p < sections
    late = in_head & (p > 0) & (pair == 0)
    sub = width // SUBS
    half = block // HALVES

    fac_copy = pltpu.make_async_copy(factor, fac, local_sem.at[0])
    dinv_copy = pltpu.make_async_copy(
        inverses.at[pl.ds(lax.rem(p, sections) * block, block)], dinv, local_sem.at[1]
    )
    dinv_copy.start()
    fac_copy.start()

    barrier = pltpu.get_barrier_semaphore()
    above, below = lax.rem(p + 2, n_prow), lax.rem(p + n_prow - 2, n_prow)
    across = (z + 1 - 2 * (z % 2)) * 2 + 1 - x
    greeted = [(row, c) for row in (above, below, beside, across)]
    greeted += [(row, mate) for row in (above, below, beside)]
    greeted += [(p, lax.rem(c + step, sections)) for step in range(1, sections)]
    for device in greeted:
        pl.semaphore_signal(barrier, inc=1, device_id=device, device_id_type=MESH)
    pl.semaphore_wait(barrier, len(greeted))

    def send(src, dst, send_sem, recv_sem, row, col):
        return pltpu.make_async_remote_copy(
            src_ref=src, dst_ref=dst, send_sem=send_sem, recv_sem=recv_sem,
            device_id=(row, col), device_id_type=MESH,
        )

    def l_piece(j, h):
        return l_in.at[j, pl.ds(h * half, half)]

    def l_copy(j, h, target, way):
        return send(
            factor.at[pl.ds(h * half, half)], l_piece(j, h), l_send.at[way, h], l_recv.at[j, h], p, target
        )

    def l_forward(j, h):
        return send(l_piece(j, h), l_piece(j, h), l_fwd.at[j, h], l_recv.at[j, h], p, j ^ 3)

    def swap(m):
        rows = pl.ds(m * piece, piece)
        return send(factor.at[rows], l_oth.at[rows], swap_send.at[m], swap_recv.at[m], p, over)

    def each_piece(body):
        for m in range(PIECES):
            if m * piece < block:
                pl.when(p >= sections)(functools.partial(body, m))
            else:
                body(m)

    for j in range(sections - 1):
        @pl.when((p > j) & in_head & (c == j))
        def _():
            for h in range(HALVES):
                l_copy(j, h, j ^ 2, 0).start()
                l_copy(j, h, j ^ 1, 1).start()

    @pl.when(jnp.logical_not(late))
    def _():
        each_piece(lambda m: swap(m).start())

    dinv_copy.wait()
    d_hi[...], d_lo[...] = split(dinv[...])
    fac_copy.wait()

    for j in range(sections - 1):
        @pl.when((p > j) & in_head & (c == j))
        def _():
            l_hi[j], l_lo[j] = split(fac[:block])

        @pl.when((p > j) & in_head & (c == (j ^ 2)))
        def _():
            for h in range(HALVES):
                l_forward(j, h).wait_recv()
                l_forward(j, h).start()
            l_hi[j], l_lo[j] = split(l_in[j])

    for j in range(sections - 1):
        @pl.when((p > j) & in_head & ((c == (j ^ 1)) | (c == (j ^ 3))))
        def _():
            for h in range(HALVES):
                l_forward(j, h).wait_recv()
            l_hi[j], l_lo[j] = split(l_in[j])

    def head_copy(s, target, col):
        rows = pl.ds(s * sub, sub)
        return send(
            x_own.at[rows], x_head.at[col, rows], head_send.at[target, s], head_recv.at[col, s], target, c
        )

    root_col = pair * 2 + p % 2
    sources = (
        (z + 1 < levels, p + 2), (z > 0, p - 2), (z >= 0, beside), (c != root_col, p),
    )

    def source_copy(s, way, target):
        rows = pl.ds(s * sub, sub)
        return send(
            x_own.at[rows], x_all.at[p // 2, parity, rows],
            source_send.at[way, s], x_recv.at[p // 2, parity, s], target, root_col,
        )

    @pl.when(in_head)
    def _():
        for s in range(SUBS):
            rows = pl.ds(s * sub, sub)
            acc[...] = rhs[rows, :block]
            for j in range(sections - 1):
                @pl.when(j < p)
                def _():
                    head_copy(s, sections - 1, j).wait_recv()
                    acc[...] -= contract(x_head[j, rows], l_hi[j], l_lo[j])
            x_own[rows] = contract(acc[...], d_hi[...], d_lo[...])
            for target in range(1, sections):
                @pl.when(p < target)
                def _():
                    head_copy(s, target, p).start()
            for way, (active, target) in enumerate(sources):
                @pl.when(active)
                def _():
                    source_copy(s, way, target).start()

            @pl.when(c == root_col)
            def _():
                x_all[p // 2, parity, rows] = x_own[rows]

    for j in range(sections - 1):
        @pl.when((p > j) & in_head & (c == j))
        def _():
            for h in range(HALVES):
                l_copy(j, h, j ^ 2, 0).wait_send()

    @pl.when(late)
    def _():
        each_piece(lambda m: swap(m).start())

    def links(slot):
        on_line = (x == parity) & (z != slot)
        return (
            (on_line & (z > slot) & (z + 1 < levels), p + 2),
            (on_line & (z < slot) & (z > 0), p - 2),
            (on_line, beside),
        )

    def tree_copy(slot, side, s, way, target):
        ref = x_all.at[slot, side, pl.ds(s * sub, sub)]
        return send(ref, ref, tree_send.at[way, slot, side, s], x_recv.at[slot, side, s], target, c)

    def own_part(slot):
        def body(m):
            rows = pl.ds(m * piece, piece)
            value = contract(x_all[slot].reshape(2 * width, block), *split(fac[rows]))
            part[m] = value.reshape(2, width, piece)

        each_piece(body)

    for slot in range(2):
        for s in range(SUBS):
            for side in range(2):
                @pl.when((p != slot * 2 + parity) | (parity != side))
                def _():
                    tree_copy(slot, side, s, 2, beside).wait_recv()

                for way, (active, target) in enumerate(links(slot)):
                    @pl.when(active)
                    def _():
                        tree_copy(slot, side, s, way, target).start()

        pl.when(pair == slot)(functools.partial(own_part, slot))

    def part_copy(m):
        return send(part.at[m, 1 - parity], fin.at[m], part_send.at[m], fin_recv.at[m], p, mate)

    def other_part(m):
        swap(m).wait_recv()
        rows = pl.ds(m * piece, piece)
        value = contract(x_all[1 - pair].reshape(2 * width, block), *split(l_oth[rows]))
        part[m] += value.reshape(2, width, piece)
        part_copy(m).start()

    each_piece(other_part)

    @pl.when(in_head)
    def _():
        out[:, :block] = x_own[...]

    def finish(m):
        cols = pl.ds(m * piece, piece)
        part_copy(m).wait_recv()
        out[:, cols] = rhs[:, cols] - (part[m, parity] + fin[m])
        part_copy(m).wait_send()
        swap(m).wait_send()

    each_piece(finish)

    for j in range(sections - 1):
        @pl.when((p > j) & in_head & (c == j))
        def _():
            for h in range(HALVES):
                l_copy(j, h, j ^ 1, 1).wait_send()

        @pl.when((p > j) & in_head & (c == (j ^ 2)))
        def _():
            for h in range(HALVES):
                l_forward(j, h).wait_send()

    @pl.when(in_head)
    def _():
        for s in range(SUBS):
            for target in range(1, sections):
                @pl.when(p < target)
                def _():
                    head_copy(s, target, p).wait_send()
            for way, (active, target) in enumerate(sources):
                @pl.when(active)
                def _():
                    source_copy(s, way, target).wait_send()

    for slot in range(2):
        for s in range(SUBS):
            for side in range(2):
                for way, (active, target) in enumerate(links(slot)):
                    @pl.when(active)
                    def _():
                        tree_copy(slot, side, s, way, target).wait_send()


def per_device(right_side, factor, inverses):
    width = right_side.shape[0]
    rows, block = factor.shape
    n_prow = lax.axis_size("prow")
    sections = lax.axis_size("pcol")
    piece = rows // PIECES
    f32, bf16 = jnp.float32, jnp.bfloat16
    vmem, dma = pltpu.VMEM, pltpu.SemaphoreType.DMA
    heads = sections - 1
    return pl.pallas_call(
        functools.partial(kernel, n_prow, sections),
        out_shape=jax.ShapeDtypeStruct(right_side.shape, f32),
        in_specs=[
            pl.BlockSpec(memory_space=pltpu.VMEM),
            pl.BlockSpec(memory_space=pl.ANY),
            pl.BlockSpec(memory_space=pl.ANY),
        ],
        out_specs=pl.BlockSpec(memory_space=pltpu.VMEM),
        scratch_shapes=[
            vmem((rows, block), f32),
            vmem((block, block), f32), vmem((block, block), bf16), vmem((block, block), bf16),
            vmem((heads, block, block), f32), vmem((heads, block, block), bf16), vmem((heads, block, block), bf16),
            vmem((rows, block), f32),
            vmem((width // SUBS, block), f32), vmem((width, block), f32),
            vmem((heads, width, block), f32), vmem((2, 2, width, block), f32),
            vmem((PIECES, 2, width, piece), f32), vmem((PIECES, width, piece), f32),
            dma((2,)), dma((2, HALVES)), dma((heads, HALVES)), dma((heads, HALVES)),
            dma((PIECES,)), dma((PIECES,)),
            dma((sections, SUBS)), dma((heads, SUBS)),
            dma((4, SUBS)), dma((3, 2, 2, SUBS)), dma((2, 2, SUBS)), dma((PIECES,)), dma((PIECES,)),
        ],
        compiler_params=pltpu.CompilerParams(
            collective_id=0, has_side_effects=True, vmem_limit_bytes=60 * 1024 * 1024
        ),
        name="solve_window",
    )(right_side, factor, inverses)


def solution(mesh):
    return jax.shard_map(
        per_device,
        mesh=mesh,
        in_specs=(P("pcol", "prow"), P("prow", "pcol"), P()),
        out_specs=P("pcol", "prow"),
        check_vma=False,
    )
```

```python
import functools

import jax
import jax.numpy as jnp
from jax import lax
from jax.experimental import pallas as pl
from jax.experimental.pallas import tpu as pltpu
from jax.sharding import PartitionSpec as P

MESH = pl.DeviceIdType.MESH
SUBS = 2
HALVES = 2
PIECES = 4


def split(value):
    high = value.astype(jnp.bfloat16)
    low = (value - high.astype(jnp.float32)).astype(jnp.bfloat16)
    return high, low


def dot_nt(left, right):
    return lax.dot_general(left, right, (((1,), (1,)), ((), ())), preferred_element_type=jnp.float32)


def contract(left, right_high, right_low):
    rows = left.shape[0]
    high, low = split(left)
    both = dot_nt(jnp.concatenate([high, low], axis=0), right_high)
    return both[:rows] + (both[rows:] + dot_nt(high, right_low))


def kernel(
    n_prow, sections, rhs, factor, inverses, out,
    fac, f_hi, f_lo, dinv, d_hi, d_lo, l_in, l_hi, l_lo, l_oth,
    acc, x_own, x_head, x_all, x_split, part, fin,
    local_sem, l_send, l_fwd, l_recv, swap_send, swap_recv, head_send, head_recv,
    mate_send, up_send, back_send, tree_send, x_recv, part_send, fin_recv,
):
    width = rhs.shape[0]
    block = factor.shape[1]
    piece = factor.shape[0] // PIECES
    p = lax.axis_index("prow")
    c = lax.axis_index("pcol")
    pair, parity = c // 2, c % 2
    mate = pair * 2 + 1 - parity
    over = (1 - pair) * 2 + parity
    z, x = p // 2, p % 2
    beside = z * 2 + 1 - x
    levels = n_prow // 2
    in_head = p < sections
    late = in_head & (p > 0) & (pair == 0)
    sub = width // SUBS
    half = block // HALVES

    fac_copy = pltpu.make_async_copy(factor, fac, local_sem.at[0])
    dinv_copy = pltpu.make_async_copy(
        inverses.at[pl.ds(lax.rem(p, sections) * block, block)], dinv, local_sem.at[1]
    )
    dinv_copy.start()
    fac_copy.start()

    barrier = pltpu.get_barrier_semaphore()
    above, below = lax.rem(p + 2, n_prow), lax.rem(p + n_prow - 2, n_prow)
    across = (z + 1 - 2 * (z % 2)) * 2 + 1 - x
    greeted = [(row, c) for row in (above, below, beside, across)]
    greeted += [(row, mate) for row in (above, below, beside, across)]
    greeted += [(p, lax.rem(c + step, sections)) for step in range(1, sections)]
    for device in greeted:
        pl.semaphore_signal(barrier, inc=1, device_id=device, device_id_type=MESH)
    pl.semaphore_wait(barrier, len(greeted))

    def send(src, dst, send_sem, recv_sem, row, col):
        return pltpu.make_async_remote_copy(
            src_ref=src, dst_ref=dst, send_sem=send_sem, recv_sem=recv_sem,
            device_id=(row, col), device_id_type=MESH,
        )

    def l_piece(j, h):
        return l_in.at[j, pl.ds(h * half, half)]

    def l_copy(j, h, target, way):
        return send(
            factor.at[pl.ds(h * half, half)], l_piece(j, h), l_send.at[way, h], l_recv.at[j, h], p, target
        )

    def l_forward(j, h):
        return send(l_piece(j, h), l_piece(j, h), l_fwd.at[j, h], l_recv.at[j, h], p, j ^ 3)

    def swap(m):
        rows = pl.ds(m * piece, piece)
        return send(factor.at[rows], l_oth.at[rows], swap_send.at[m], swap_recv.at[m], p, over)

    def each_piece(body):
        for m in range(PIECES):
            if m * piece < block:
                pl.when(p >= sections)(functools.partial(body, m))
            else:
                body(m)

    for j in range(sections - 1):
        @pl.when((p > j) & in_head & (c == j))
        def _():
            for h in range(HALVES):
                l_copy(j, h, j ^ 2, 0).start()
                l_copy(j, h, j ^ 1, 1).start()

    @pl.when(jnp.logical_not(late))
    def _():
        each_piece(lambda m: swap(m).start())

    dinv_copy.wait()
    d_hi[...], d_lo[...] = split(dinv[...])
    fac_copy.wait()

    for j in range(sections - 1):
        @pl.when((p > j) & in_head & (c == j))
        def _():
            l_hi[j], l_lo[j] = split(fac[:block])

        @pl.when((p > j) & in_head & (c == (j ^ 2)))
        def _():
            for h in range(HALVES):
                l_forward(j, h).wait_recv()
                l_forward(j, h).start()
            l_hi[j], l_lo[j] = split(l_in[j])

    for j in range(sections - 1):
        @pl.when((p > j) & in_head & ((c == (j ^ 1)) | (c == (j ^ 3))))
        def _():
            for h in range(HALVES):
                l_forward(j, h).wait_recv()
            l_hi[j], l_lo[j] = split(l_in[j])

    def head_copy(s, target, col):
        rows = pl.ds(s * sub, sub)
        return send(
            x_own.at[rows], x_head.at[col, rows], head_send.at[target, s], head_recv.at[col, s], target, c
        )

    def publish_copy(ref, k, s, sems, row):
        rows = pl.ds(s * sub, sub)
        return send(
            ref.at[rows], x_all.at[k // 2, parity, rows],
            sems, x_recv.at[k // 2, parity, s], row, pair * 2 + k % 2,
        )

    def publish(ref, k, s, act):
        pl.when(parity != k % 2)(lambda: act(publish_copy(ref, k, s, mate_send.at[k, s], p)))
        pl.when((p == 2 + k % 2) & (z + 1 < levels))(
            lambda: act(publish_copy(ref, k, s, up_send.at[k, s], p + 2))
        )

    def keep(ref, k, s):
        rows = pl.ds(s * sub, sub)

        @pl.when(parity == k % 2)
        def _():
            x_all[k // 2, parity, rows] = ref[rows]

    def go_back(s, act):
        for row in range(sections - 1):
            pl.when(row < p)(lambda: act(publish_copy(x_own, p, s, back_send.at[row, s], row)))

    start = lambda copy: copy.start()
    drain = lambda copy: copy.wait_send()

    @pl.when(in_head)
    def _():
        for s in range(SUBS):
            rows = pl.ds(s * sub, sub)
            acc[...] = rhs[rows, :block]
            for j in range(sections - 1):
                @pl.when(j < p)
                def _():
                    head_copy(s, sections - 1, j).wait_recv()
                    publish(x_head.at[j], j, s, start)
                    acc[...] -= contract(x_head[j, rows], l_hi[j], l_lo[j])
            x_own[rows] = contract(acc[...], d_hi[...], d_lo[...])
            for target in range(1, sections):
                @pl.when((p == target - 1) | ((p < target) & (target < sections - 1)))
                def _():
                    head_copy(s, target, p).start()
            publish(x_own, p, s, start)
            go_back(s, start)
            keep(x_own, p, s)
            for j in range(sections - 1):
                pl.when(j < p)(lambda: keep(x_head.at[j], j, s))

        @pl.when(p < sections - 2)
        def _():
            for s in range(SUBS):
                head_copy(s, sections - 1, p).start()

    for j in range(sections - 1):
        @pl.when((p > j) & in_head & (c == j))
        def _():
            for h in range(HALVES):
                l_copy(j, h, j ^ 2, 0).wait_send()

    @pl.when(late)
    def _():
        each_piece(lambda m: swap(m).start())

    for m in range(PIECES):
        rows = pl.ds(m * piece, piece)
        f_hi[rows], f_lo[rows] = split(fac[rows])

    links = (
        (jnp.logical_not(in_head) & (x == parity) & (z + 1 < levels), p + 2),
        (jnp.logical_not(in_head) & (x == parity), beside),
    )

    def tree_copy(slot, side, s, way, target):
        ref = x_all.at[slot, side, pl.ds(s * sub, sub)]
        return send(ref, ref, tree_send.at[way, slot, side, s], x_recv.at[slot, side, s], target, c)

    def spread(slot):
        kept = in_head & (p >= slot * 2 + parity)
        for s in range(SUBS):
            for side in range(2):
                @pl.when(jnp.logical_not(kept & (parity == side)))
                def _():
                    tree_copy(slot, side, s, 1, beside).wait_recv()

                for way, (active, target) in enumerate(links):
                    @pl.when(active)
                    def _():
                        tree_copy(slot, side, s, way, target).start()
        high, low = split(x_all[slot].reshape(2 * width, block))
        x_split[slot, :2 * width] = high
        x_split[slot, 2 * width:] = low

    def product(slot, right_high, right_low):
        both = dot_nt(x_split[slot], right_high)
        low = dot_nt(x_split[slot, :2 * width], right_low)
        return (both[:2 * width] + (both[2 * width:] + low)).reshape(2, width, piece)

    def own(m, slot):
        rows = pl.ds(m * piece, piece)
        return product(slot, f_hi[rows], f_lo[rows])

    def other(m, slot):
        swap(m).wait_recv()
        return product(slot, *split(l_oth[pl.ds(m * piece, piece)]))

    def part_copy(m):
        return send(part.at[m, 1 - parity], fin.at[m], part_send.at[m], fin_recv.at[m], p, mate)

    def first_own(slot, m):
        part[m] = own(m, slot)

    def first_other(m):
        if m < PIECES - 1:
            part[m] = other(m, 0)

    def then_own(m):
        if m < PIECES - 1:
            part[m] += own(m, 1)
        else:
            part[m] = own(m, 1)
            part[m] += other(m, 0)
        part_copy(m).start()

    def then_other(slot, m):
        part[m] += other(m, slot)
        part_copy(m).start()

    early = (pair == 1) & (in_head | (x != parity))
    spread(0)
    pl.when(pair == 0)(lambda: each_piece(functools.partial(first_own, 0)))
    pl.when(early)(lambda: each_piece(first_other))
    spread(1)
    pl.when(pair == 0)(lambda: each_piece(functools.partial(then_other, 1)))
    pl.when(early)(lambda: each_piece(then_own))

    @pl.when((pair == 1) & jnp.logical_not(early))
    def _():
        each_piece(functools.partial(first_own, 1))
        each_piece(functools.partial(then_other, 0))

    @pl.when(in_head)
    def _():
        out[:, :block] = x_own[...]

    def finish(m):
        cols = pl.ds(m * piece, piece)
        part_copy(m).wait_recv()
        out[:, cols] = rhs[:, cols] - (part[m, parity] + fin[m])
        part_copy(m).wait_send()
        swap(m).wait_send()

    each_piece(finish)

    for j in range(sections - 1):
        @pl.when((p > j) & in_head & (c == j))
        def _():
            for h in range(HALVES):
                l_copy(j, h, j ^ 1, 1).wait_send()

        @pl.when((p > j) & in_head & (c == (j ^ 2)))
        def _():
            for h in range(HALVES):
                l_forward(j, h).wait_send()

    @pl.when(in_head)
    def _():
        for s in range(SUBS):
            for target in range(1, sections):
                @pl.when(p < target)
                def _():
                    head_copy(s, target, p).wait_send()
            publish(x_own, p, s, drain)
            go_back(s, drain)
            for j in range(sections - 1):
                pl.when(j < p)(lambda: publish(x_head.at[j], j, s, drain))

    for slot in range(2):
        for s in range(SUBS):
            for side in range(2):
                for way, (active, target) in enumerate(links):
                    @pl.when(active)
                    def _():
                        tree_copy(slot, side, s, way, target).wait_send()


def per_device(right_side, factor, inverses):
    width = right_side.shape[0]
    rows, block = factor.shape
    n_prow = lax.axis_size("prow")
    sections = lax.axis_size("pcol")
    piece = rows // PIECES
    f32, bf16 = jnp.float32, jnp.bfloat16
    vmem, dma = pltpu.VMEM, pltpu.SemaphoreType.DMA
    heads = sections - 1
    return pl.pallas_call(
        functools.partial(kernel, n_prow, sections),
        out_shape=jax.ShapeDtypeStruct(right_side.shape, f32),
        in_specs=[
            pl.BlockSpec(memory_space=pltpu.VMEM),
            pl.BlockSpec(memory_space=pl.ANY),
            pl.BlockSpec(memory_space=pl.ANY),
        ],
        out_specs=pl.BlockSpec(memory_space=pltpu.VMEM),
        scratch_shapes=[
            vmem((rows, block), f32), vmem((rows, block), bf16), vmem((rows, block), bf16),
            vmem((block, block), f32), vmem((block, block), bf16), vmem((block, block), bf16),
            vmem((heads, block, block), f32), vmem((heads, block, block), bf16), vmem((heads, block, block), bf16),
            vmem((rows, block), f32),
            vmem((width // SUBS, block), f32), vmem((width, block), f32),
            vmem((heads, width, block), f32), vmem((2, 2, width, block), f32),
            vmem((2, 4 * width, block), bf16),
            vmem((PIECES, 2, width, piece), f32), vmem((PIECES, width, piece), f32),
            dma((2,)), dma((2, HALVES)), dma((heads, HALVES)), dma((heads, HALVES)),
            dma((PIECES,)), dma((PIECES,)),
            dma((sections, SUBS)), dma((heads, SUBS)),
            dma((sections, SUBS)), dma((sections, SUBS)), dma((heads, SUBS)),
            dma((2, 2, 2, SUBS)), dma((2, 2, SUBS)), dma((PIECES,)), dma((PIECES,)),
        ],
        compiler_params=pltpu.CompilerParams(
            collective_id=0, has_side_effects=True, vmem_limit_bytes=60 * 1024 * 1024
        ),
        name="solve_window",
    )(right_side, factor, inverses)


def solution(mesh):
    return jax.shard_map(
        per_device,
        mesh=mesh,
        in_specs=(P("pcol", "prow"), P("prow", "pcol"), P()),
        out_specs=P("pcol", "prow"),
        check_vma=False,
    )
```

```python
import functools

import jax
import jax.numpy as jnp
from jax import lax
from jax.experimental import pallas as pl
from jax.experimental.pallas import tpu as pltpu
from jax.sharding import PartitionSpec as P

MESH = pl.DeviceIdType.MESH
SUBS = 2
HALVES = 2
PIECES = 4


def split(value):
    high = value.astype(jnp.bfloat16)
    low = (value - high.astype(jnp.float32)).astype(jnp.bfloat16)
    return high, low


def dot_nt(left, right):
    return lax.dot_general(left, right, (((1,), (1,)), ((), ())), preferred_element_type=jnp.float32)


def dot_nn(left, right):
    return lax.dot_general(left, right, (((1,), (0,)), ((), ())), preferred_element_type=jnp.float32)


def contract(left, right_high, right_low):
    rows = left.shape[0]
    high, low = split(left)
    both = dot_nt(jnp.concatenate([high, low], axis=0), right_high)
    return both[:rows] + (both[rows:] + dot_nt(high, right_low))


def kernel(
    n_prow, sections, rhs, factor, inverses, out,
    fac, f_hi, f_lo, dinv, d_hi, d_lo, l_in, l_hi, l_lo, m_hi, m_lo, l_oth,
    acc, x_own, x_head, x_all, x_split, part, fin,
    local_sem, l_send, l_fwd, l_recv, swap_send, swap_recv, head_send, head_recv,
    mate_send, up_send, back_send, tree_send, x_recv, part_send, fin_recv,
):
    width = rhs.shape[0]
    block = factor.shape[1]
    piece = factor.shape[0] // PIECES
    p = lax.axis_index("prow")
    c = lax.axis_index("pcol")
    pair, parity = c // 2, c % 2
    mate = pair * 2 + 1 - parity
    over = (1 - pair) * 2 + parity
    z, x = p // 2, p % 2
    beside = z * 2 + 1 - x
    levels = n_prow // 2
    in_head = p < sections
    last = sections - 1
    at_once = (p >= sections) | ((p == last - 1) & (pair == 1))
    sub = width // SUBS
    half = block // HALVES

    fac_copy = pltpu.make_async_copy(factor, fac, local_sem.at[0])
    dinv_copy = pltpu.make_async_copy(
        inverses.at[pl.ds(lax.rem(p, sections) * block, block)], dinv, local_sem.at[1]
    )
    dinv_copy.start()
    fac_copy.start()

    barrier = pltpu.get_barrier_semaphore()
    above, below = lax.rem(p + 2, n_prow), lax.rem(p + n_prow - 2, n_prow)
    across = (z + 1 - 2 * (z % 2)) * 2 + 1 - x
    greeted = [(row, c) for row in (above, below, beside, across)]
    greeted += [(row, mate) for row in (above, below, beside, across)]
    greeted += [(p, lax.rem(c + step, sections)) for step in range(1, sections)]
    for device in greeted:
        pl.semaphore_signal(barrier, inc=1, device_id=device, device_id_type=MESH)
    pl.semaphore_wait(barrier, len(greeted))

    def send(src, dst, send_sem, recv_sem, row, col):
        return pltpu.make_async_remote_copy(
            src_ref=src, dst_ref=dst, send_sem=send_sem, recv_sem=recv_sem,
            device_id=(row, col), device_id_type=MESH,
        )

    def l_piece(j, h):
        return l_in.at[j, pl.ds(h * half, half)]

    def l_copy(j, h, target, way):
        return send(
            factor.at[pl.ds(h * half, half)], l_piece(j, h), l_send.at[way, h], l_recv.at[j, h], p, target
        )

    def l_forward(j, h):
        return send(l_piece(j, h), l_piece(j, h), l_fwd.at[j, h], l_recv.at[j, h], p, j ^ 3)

    def swap(m):
        rows = pl.ds(m * piece, piece)
        return send(factor.at[rows], l_oth.at[rows], swap_send.at[m], swap_recv.at[m], p, over)

    def each_piece(body):
        for m in range(PIECES):
            if m * piece < block:
                pl.when(p >= sections)(functools.partial(body, m))
            else:
                body(m)

    for j in range(sections - 1):
        @pl.when((p > j) & in_head & (c == j))
        def _():
            for h in range(HALVES):
                l_copy(j, h, j ^ 2, 0).start()
                l_copy(j, h, j ^ 1, 1).start()

    @pl.when(at_once)
    def _():
        each_piece(lambda m: swap(m).start())

    dinv_copy.wait()
    d_hi[...], d_lo[...] = split(dinv[...])
    fac_copy.wait()

    for j in range(sections - 1):
        @pl.when((p > j) & in_head & (c == j))
        def _():
            l_hi[j], l_lo[j] = split(fac[:block])

        @pl.when((p > j) & in_head & (c == (j ^ 2)))
        def _():
            for h in range(HALVES):
                l_forward(j, h).wait_recv()
                l_forward(j, h).start()
            l_hi[j], l_lo[j] = split(l_in[j])

    for j in range(sections - 1):
        @pl.when((p > j) & in_head & ((c == (j ^ 1)) | (c == (j ^ 3))))
        def _():
            for h in range(HALVES):
                l_forward(j, h).wait_recv()
            l_hi[j], l_lo[j] = split(l_in[j])

    def head_copy(s, target, col):
        rows = pl.ds(s * sub, sub)
        return send(
            x_own.at[rows], x_head.at[col, rows], head_send.at[target, s], head_recv.at[col, s], target, c
        )

    def publish_copy(ref, k, s, sems, row):
        rows = pl.ds(s * sub, sub)
        return send(
            ref.at[rows], x_all.at[k // 2, parity, rows],
            sems, x_recv.at[k // 2, parity, s], row, pair * 2 + k % 2,
        )

    def publish(ref, k, s, act):
        pl.when(parity != k % 2)(lambda: act(publish_copy(ref, k, s, mate_send.at[k, s], p)))
        pl.when((p == 2 + k % 2) & (z + 1 < levels))(
            lambda: act(publish_copy(ref, k, s, up_send.at[k, s], p + 2))
        )

    def keep(ref, k, s):
        rows = pl.ds(s * sub, sub)

        @pl.when(parity == k % 2)
        def _():
            x_all[k // 2, parity, rows] = ref[rows]

    def go_back(s, act):
        for row in range(sections - 1):
            pl.when(row < p)(lambda: act(publish_copy(x_own, p, s, back_send.at[row, s], row)))

    start = lambda copy: copy.start()
    drain = lambda copy: copy.wait_send()

    def swap_late():
        for j in range(sections - 1):
            @pl.when((p > j) & (c == j))
            def _():
                for h in range(HALVES):
                    l_copy(j, h, j ^ 2, 0).wait_send()
        each_piece(lambda m: swap(m).start())

    pl.when(p == last)(swap_late)

    @pl.when(in_head)
    def _():
        acc[...] = rhs[:, :block]
        for j in range(sections - 1):
            @pl.when(p == j + 1)
            def _():
                both = dot_nn(jnp.concatenate([d_hi[...], d_lo[...]], axis=0), l_hi[j])
                chain = both[:block] + (both[block:] + dot_nn(d_hi[...], l_lo[j]))
                m_hi[...], m_lo[...] = split(chain)

        for j in range(sections - 2):
            @pl.when(p > j + 1)
            def _():
                for s in range(SUBS):
                    head_copy(s, last, j).wait_recv()
                    publish(x_head.at[j], j, s, start)
                acc[...] -= contract(x_head[j], l_hi[j], l_lo[j])

        acc[...] = contract(acc[...], d_hi[...], d_lo[...])
        for s in range(SUBS):
            rows = pl.ds(s * sub, sub)
            x_own[rows] = acc[rows]
            for j in range(sections - 1):
                @pl.when(p == j + 1)
                def _():
                    head_copy(s, last, j).wait_recv()
                    x_own[rows] = acc[rows] - contract(x_head[j, rows], m_hi[...], m_lo[...])
            for target in range(1, sections):
                @pl.when((p == target - 1) | ((p < target) & (target < sections - 1)))
                def _():
                    head_copy(s, target, p).start()
            publish(x_own, p, s, start)
            go_back(s, start)
            for j in range(sections - 1):
                @pl.when(p == j + 1)
                def _():
                    publish(x_head.at[j], j, s, start)

        @pl.when(p < sections - 2)
        def _():
            for s in range(SUBS):
                head_copy(s, sections - 1, p).start()

        for s in range(SUBS):
            keep(x_own, p, s)
            for j in range(sections - 1):
                pl.when(j < p)(lambda: keep(x_head.at[j], j, s))

    @pl.when(jnp.logical_not(at_once) & (p != last))
    def _():
        swap_late()

    for m in range(PIECES):
        rows = pl.ds(m * piece, piece)
        f_hi[rows], f_lo[rows] = split(fac[rows])

    links = (
        (jnp.logical_not(in_head) & (x == parity) & (z + 1 < levels), p + 2),
        (jnp.logical_not(in_head) & (x == parity), beside),
    )

    def tree_copy(slot, side, s, way, target):
        ref = x_all.at[slot, side, pl.ds(s * sub, sub)]
        return send(ref, ref, tree_send.at[way, slot, side, s], x_recv.at[slot, side, s], target, c)

    def spread(slot):
        kept = in_head & (p >= slot * 2 + parity)
        for s in range(SUBS):
            for side in range(2):
                @pl.when(jnp.logical_not(kept & (parity == side)))
                def _():
                    tree_copy(slot, side, s, 1, beside).wait_recv()

                for way, (active, target) in enumerate(links):
                    @pl.when(active)
                    def _():
                        tree_copy(slot, side, s, way, target).start()
        high, low = split(x_all[slot].reshape(2 * width, block))
        x_split[slot, :2 * width] = high
        x_split[slot, 2 * width:] = low

    def product(slot, right_high, right_low):
        both = dot_nt(x_split[slot], right_high)
        low = dot_nt(x_split[slot, :2 * width], right_low)
        return (both[:2 * width] + (both[2 * width:] + low)).reshape(2, width, piece)

    def own(m, slot):
        rows = pl.ds(m * piece, piece)
        return product(slot, f_hi[rows], f_lo[rows])

    def other(m, slot):
        swap(m).wait_recv()
        return product(slot, *split(l_oth[pl.ds(m * piece, piece)]))

    def part_copy(m):
        return send(part.at[m, 1 - parity], fin.at[m], part_send.at[m], fin_recv.at[m], p, mate)

    def first_own(slot, m):
        part[m] = own(m, slot)

    def first_other(m):
        if m < PIECES - 1:
            part[m] = other(m, 0)

    def then_own(m):
        if m < PIECES - 1:
            part[m] += own(m, 1)
        else:
            part[m] = own(m, 1)
            part[m] += other(m, 0)
        part_copy(m).start()

    def then_other(slot, m):
        part[m] += other(m, slot)
        part_copy(m).start()

    early = (pair == 1) & (in_head | (x != parity))
    spread(0)
    pl.when(pair == 0)(lambda: each_piece(functools.partial(first_own, 0)))
    pl.when(early)(lambda: each_piece(first_other))
    spread(1)
    pl.when(pair == 0)(lambda: each_piece(functools.partial(then_other, 1)))
    pl.when(early)(lambda: each_piece(then_own))

    @pl.when((pair == 1) & jnp.logical_not(early))
    def _():
        each_piece(functools.partial(first_own, 1))
        each_piece(functools.partial(then_other, 0))

    @pl.when(in_head)
    def _():
        out[:, :block] = x_own[...]

    def finish(m):
        cols = pl.ds(m * piece, piece)
        part_copy(m).wait_recv()
        out[:, cols] = rhs[:, cols] - (part[m, parity] + fin[m])
        part_copy(m).wait_send()
        swap(m).wait_send()

    each_piece(finish)

    for j in range(sections - 1):
        @pl.when((p > j) & in_head & (c == j))
        def _():
            for h in range(HALVES):
                l_copy(j, h, j ^ 1, 1).wait_send()

        @pl.when((p > j) & in_head & (c == (j ^ 2)))
        def _():
            for h in range(HALVES):
                l_forward(j, h).wait_send()

    @pl.when(in_head)
    def _():
        for s in range(SUBS):
            for target in range(1, sections):
                @pl.when(p < target)
                def _():
                    head_copy(s, target, p).wait_send()
            publish(x_own, p, s, drain)
            go_back(s, drain)
            for j in range(sections - 1):
                pl.when(j < p)(lambda: publish(x_head.at[j], j, s, drain))

    for slot in range(2):
        for s in range(SUBS):
            for side in range(2):
                for way, (active, target) in enumerate(links):
                    @pl.when(active)
                    def _():
                        tree_copy(slot, side, s, way, target).wait_send()


def per_device(right_side, factor, inverses):
    width = right_side.shape[0]
    rows, block = factor.shape
    n_prow = lax.axis_size("prow")
    sections = lax.axis_size("pcol")
    piece = rows // PIECES
    f32, bf16 = jnp.float32, jnp.bfloat16
    vmem, dma = pltpu.VMEM, pltpu.SemaphoreType.DMA
    heads = sections - 1
    return pl.pallas_call(
        functools.partial(kernel, n_prow, sections),
        out_shape=jax.ShapeDtypeStruct(right_side.shape, f32),
        in_specs=[
            pl.BlockSpec(memory_space=pltpu.VMEM),
            pl.BlockSpec(memory_space=pl.ANY),
            pl.BlockSpec(memory_space=pl.ANY),
        ],
        out_specs=pl.BlockSpec(memory_space=pltpu.VMEM),
        scratch_shapes=[
            vmem((rows, block), f32), vmem((rows, block), bf16), vmem((rows, block), bf16),
            vmem((block, block), f32), vmem((block, block), bf16), vmem((block, block), bf16),
            vmem((heads, block, block), f32), vmem((heads, block, block), bf16), vmem((heads, block, block), bf16),
            vmem((block, block), bf16), vmem((block, block), bf16), vmem((rows, block), f32),
            vmem((width, block), f32), vmem((width, block), f32),
            vmem((heads, width, block), f32), vmem((2, 2, width, block), f32),
            vmem((2, 4 * width, block), bf16),
            vmem((PIECES, 2, width, piece), f32), vmem((PIECES, width, piece), f32),
            dma((2,)), dma((2, HALVES)), dma((heads, HALVES)), dma((heads, HALVES)),
            dma((PIECES,)), dma((PIECES,)),
            dma((sections, SUBS)), dma((heads, SUBS)),
            dma((sections, SUBS)), dma((sections, SUBS)), dma((heads, SUBS)),
            dma((2, 2, 2, SUBS)), dma((2, 2, SUBS)), dma((PIECES,)), dma((PIECES,)),
        ],
        compiler_params=pltpu.CompilerParams(
            collective_id=0, has_side_effects=True, vmem_limit_bytes=60 * 1024 * 1024
        ),
        name="solve_window",
    )(right_side, factor, inverses)


def solution(mesh):
    return jax.shard_map(
        per_device,
        mesh=mesh,
        in_specs=(P("pcol", "prow"), P("prow", "pcol"), P()),
        out_specs=P("pcol", "prow"),
        check_vma=False,
    )
```

```python
import functools

import jax
import jax.numpy as jnp
from jax import lax
from jax.experimental import pallas as pl
from jax.experimental.pallas import tpu as pltpu
from jax.sharding import PartitionSpec as P

MESH = pl.DeviceIdType.MESH
SUBS = 2
HALVES = 2
PIECES = 4


def split(value):
    high = value.astype(jnp.bfloat16)
    low = (value - high.astype(jnp.float32)).astype(jnp.bfloat16)
    return high, low


def dot_nt(left, right):
    return lax.dot_general(left, right, (((1,), (1,)), ((), ())), preferred_element_type=jnp.float32)


def dot_nn(left, right):
    return lax.dot_general(left, right, (((1,), (0,)), ((), ())), preferred_element_type=jnp.float32)


def contract(left, right_high, right_low):
    rows = left.shape[0]
    high, low = split(left)
    both = dot_nt(jnp.concatenate([high, low], axis=0), right_high)
    return both[:rows] + (both[rows:] + dot_nt(high, right_low))


def kernel(
    n_prow, sections, rhs, factor, inverses, out,
    fac, f_hi, f_lo, dinv, d_hi, d_lo, l_in, l_hi, l_lo, m_hi, m_lo, l_oth,
    acc, x_own, x_head, x_all, x_split, part, fin,
    local_sem, l_send, l_fwd, l_recv, swap_send, swap_recv, head_send, head_recv,
    mate_send, up_send, back_send, tree_send, x_recv, part_send, fin_recv,
):
    width = rhs.shape[0]
    block = factor.shape[1]
    piece = factor.shape[0] // PIECES
    p = lax.axis_index("prow")
    c = lax.axis_index("pcol")
    pair, parity = c // 2, c % 2
    mate = pair * 2 + 1 - parity
    over = (1 - pair) * 2 + parity
    z, x = p // 2, p % 2
    beside = z * 2 + 1 - x
    levels = n_prow // 2
    in_head = p < sections
    last = sections - 1
    folded = (pair == 0) | (p == last)
    at_once = (p >= sections) | ((p == last - 1) & (pair == 1))
    sub = width // SUBS
    half = block // HALVES

    fac_copy = pltpu.make_async_copy(factor, fac, local_sem.at[0])
    dinv_copy = pltpu.make_async_copy(
        inverses.at[pl.ds(lax.rem(p, sections) * block, block)], dinv, local_sem.at[1]
    )
    dinv_copy.start()
    fac_copy.start()

    barrier = pltpu.get_barrier_semaphore()
    above, below = lax.rem(p + 2, n_prow), lax.rem(p + n_prow - 2, n_prow)
    across = (z + 1 - 2 * (z % 2)) * 2 + 1 - x
    greeted = [(row, c) for row in (above, below, beside, across)]
    greeted += [(row, mate) for row in (above, below, beside, across)]
    greeted += [(p, lax.rem(c + step, sections)) for step in range(1, sections)]
    for device in greeted:
        pl.semaphore_signal(barrier, inc=1, device_id=device, device_id_type=MESH)
    pl.semaphore_wait(barrier, len(greeted))

    def send(src, dst, send_sem, recv_sem, row, col):
        return pltpu.make_async_remote_copy(
            src_ref=src, dst_ref=dst, send_sem=send_sem, recv_sem=recv_sem,
            device_id=(row, col), device_id_type=MESH,
        )

    def l_piece(j, h):
        return l_in.at[j, pl.ds(h * half, half)]

    def l_copy(j, h, target, way):
        return send(
            factor.at[pl.ds(h * half, half)], l_piece(j, h), l_send.at[way, h], l_recv.at[j, h], p, target
        )

    def l_forward(j, h):
        return send(l_piece(j, h), l_piece(j, h), l_fwd.at[j, h], l_recv.at[j, h], p, j ^ 3)

    def swap(m):
        rows = pl.ds(m * piece, piece)
        return send(factor.at[rows], l_oth.at[rows], swap_send.at[m], swap_recv.at[m], p, over)

    def each_piece(body):
        for m in range(PIECES):
            if m * piece < block:
                pl.when(p >= sections)(functools.partial(body, m))
            else:
                body(m)

    for j in range(sections - 1):
        @pl.when((p > j) & in_head & (c == j))
        def _():
            for h in range(HALVES):
                l_copy(j, h, j ^ 2, 0).start()
                l_copy(j, h, j ^ 1, 1).start()

    first, rest = range(PIECES // 2), range(PIECES // 2, PIECES)

    @pl.when(at_once)
    def _():
        for m in first:
            pl.when(p >= sections)(lambda: swap(m).start())
        for m in rest:
            pl.when(p < sections)(lambda: swap(m).start())

    dinv_copy.wait()
    d_hi[...], d_lo[...] = split(dinv[...])
    fac_copy.wait()

    for j in range(sections - 1):
        @pl.when((p > j) & in_head & (c == j))
        def _():
            l_hi[j], l_lo[j] = split(fac[:block])

        @pl.when((p > j) & in_head & (c == (j ^ 2)))
        def _():
            for h in range(HALVES):
                l_forward(j, h).wait_recv()
                l_forward(j, h).start()
            l_hi[j], l_lo[j] = split(l_in[j])

    for j in range(sections - 1):
        @pl.when((p > j) & in_head & ((c == (j ^ 1)) | (c == (j ^ 3))))
        def _():
            for h in range(HALVES):
                l_forward(j, h).wait_recv()
            l_hi[j], l_lo[j] = split(l_in[j])

    def head_copy(s, target, col):
        rows = pl.ds(s * sub, sub)
        return send(
            x_own.at[rows], x_head.at[col, rows], head_send.at[target, s], head_recv.at[col, s], target, c
        )

    def publish_copy(ref, k, s, sems, row):
        rows = pl.ds(s * sub, sub)
        return send(
            ref.at[rows], x_all.at[k // 2, parity, rows],
            sems, x_recv.at[k // 2, parity, s], row, pair * 2 + k % 2,
        )

    def publish(ref, k, s, act):
        pl.when(parity != k % 2)(lambda: act(publish_copy(ref, k, s, mate_send.at[k, s], p)))
        pl.when((p == 2 + k % 2) & (z + 1 < levels))(
            lambda: act(publish_copy(ref, k, s, up_send.at[k, s], p + 2))
        )

    def keep(ref, k, s):
        rows = pl.ds(s * sub, sub)

        @pl.when(parity == k % 2)
        def _():
            x_all[k // 2, parity, rows] = ref[rows]

    def go_back(s, act):
        for row in range(sections - 1):
            pl.when(row < p)(lambda: act(publish_copy(x_own, p, s, back_send.at[row, s], row)))

    start = lambda copy: copy.start()
    drain = lambda copy: copy.wait_send()

    def swap_late():
        for j in range(sections - 1):
            @pl.when((p > j) & (c == j))
            def _():
                for h in range(HALVES):
                    l_copy(j, h, j ^ 2, 0).wait_send()
        each_piece(lambda m: swap(m).start())

    pl.when(p == last)(swap_late)

    @pl.when(in_head)
    def _():
        acc[...] = rhs[:, :block]
        for j in range(sections - 1):
            @pl.when((p == j + 1) & folded)
            def _():
                both = dot_nn(jnp.concatenate([d_hi[...], d_lo[...]], axis=0), l_hi[j])
                chain = both[:block] + (both[block:] + dot_nn(d_hi[...], l_lo[j]))
                m_hi[...], m_lo[...] = split(chain)

        for j in range(sections - 1):
            @pl.when((p > j + 1) | ((p == j + 1) & jnp.logical_not(folded)))
            def _():
                for s in range(SUBS):
                    head_copy(s, last, j).wait_recv()
                    publish(x_head.at[j], j, s, start)
                acc[...] -= contract(x_head[j], l_hi[j], l_lo[j])

        acc[...] = contract(acc[...], d_hi[...], d_lo[...])
        for s in range(SUBS):
            rows = pl.ds(s * sub, sub)
            x_own[rows] = acc[rows]
            for j in range(sections - 1):
                @pl.when((p == j + 1) & folded)
                def _():
                    head_copy(s, last, j).wait_recv()
                    x_own[rows] = acc[rows] - contract(x_head[j, rows], m_hi[...], m_lo[...])
            for target in range(1, sections):
                @pl.when((p == target - 1) | ((p < target) & (target < sections - 1)))
                def _():
                    head_copy(s, target, p).start()
            publish(x_own, p, s, start)
            go_back(s, start)
            for j in range(sections - 1):
                @pl.when((p == j + 1) & folded)
                def _():
                    publish(x_head.at[j], j, s, start)

        @pl.when(p < sections - 2)
        def _():
            for s in range(SUBS):
                head_copy(s, sections - 1, p).start()

        for s in range(SUBS):
            keep(x_own, p, s)
            for j in range(sections - 1):
                pl.when(j < p)(lambda: keep(x_head.at[j], j, s))

    @pl.when(jnp.logical_not(at_once) & (p != last))
    def _():
        swap_late()

    for m in range(PIECES):
        rows = pl.ds(m * piece, piece)
        f_hi[rows], f_lo[rows] = split(fac[rows])

    links = (
        (jnp.logical_not(in_head) & (x == parity) & (z + 1 < levels), p + 2),
        (jnp.logical_not(in_head) & (x == parity), beside),
    )

    def tree_copy(slot, side, s, way, target):
        ref = x_all.at[slot, side, pl.ds(s * sub, sub)]
        return send(ref, ref, tree_send.at[way, slot, side, s], x_recv.at[slot, side, s], target, c)

    def spread(slot):
        kept = in_head & (p >= slot * 2 + parity)
        for s in range(SUBS):
            for side in range(2):
                @pl.when(jnp.logical_not(kept & (parity == side)))
                def _():
                    tree_copy(slot, side, s, 1, beside).wait_recv()

                for way, (active, target) in enumerate(links):
                    @pl.when(active)
                    def _():
                        tree_copy(slot, side, s, way, target).start()
        high, low = split(x_all[slot].reshape(2 * width, block))
        x_split[slot, :2 * width] = high
        x_split[slot, 2 * width:] = low

    def product(slot, right_high, right_low):
        both = dot_nt(x_split[slot], right_high)
        low = dot_nt(x_split[slot, :2 * width], right_low)
        return (both[:2 * width] + (both[2 * width:] + low)).reshape(2, width, piece)

    def own(m, slot):
        rows = pl.ds(m * piece, piece)
        return product(slot, f_hi[rows], f_lo[rows])

    def other(m, slot):
        swap(m).wait_recv()
        return product(slot, *split(l_oth[pl.ds(m * piece, piece)]))

    def part_copy(m):
        return send(part.at[m, 1 - parity], fin.at[m], part_send.at[m], fin_recv.at[m], p, mate)

    def first_own(slot, m):
        part[m] = own(m, slot)

    def then_other(slot, m):
        part[m] += other(m, slot)
        part_copy(m).start()

    def then_own(m):
        if m in first:
            part[m] += own(m, 1)
            part_copy(m).start()
        else:
            part[m] = own(m, 1)

    @pl.when(p >= sections)
    def _():
        for m in first:
            swap(m).wait_send()
            swap(m + PIECES // 2).start()

    spread(0)
    pl.when(pair == 0)(lambda: each_piece(functools.partial(first_own, 0)))

    @pl.when((pair == 1) & (p >= sections))
    def _():
        for m in first:
            part[m] = other(m, 0)

    spread(1)
    pl.when(pair == 0)(lambda: each_piece(functools.partial(then_other, 1)))

    @pl.when(pair == 1)
    def _():
        each_piece(then_own)
        for m in rest:
            then_other(0, m)

    @pl.when(in_head)
    def _():
        out[:, :block] = x_own[...]

    def finish(m):
        cols = pl.ds(m * piece, piece)
        part_copy(m).wait_recv()
        out[:, cols] = rhs[:, cols] - (part[m, parity] + fin[m])
        part_copy(m).wait_send()
        if m in rest:
            swap(m).wait_send()

    each_piece(finish)

    for j in range(sections - 1):
        @pl.when((p > j) & in_head & (c == j))
        def _():
            for h in range(HALVES):
                l_copy(j, h, j ^ 1, 1).wait_send()

        @pl.when((p > j) & in_head & (c == (j ^ 2)))
        def _():
            for h in range(HALVES):
                l_forward(j, h).wait_send()

    @pl.when(in_head)
    def _():
        for s in range(SUBS):
            for target in range(1, sections):
                @pl.when(p < target)
                def _():
                    head_copy(s, target, p).wait_send()
            publish(x_own, p, s, drain)
            go_back(s, drain)
            for j in range(sections - 1):
                pl.when(j < p)(lambda: publish(x_head.at[j], j, s, drain))

    for slot in range(2):
        for s in range(SUBS):
            for side in range(2):
                for way, (active, target) in enumerate(links):
                    @pl.when(active)
                    def _():
                        tree_copy(slot, side, s, way, target).wait_send()


def per_device(right_side, factor, inverses):
    width = right_side.shape[0]
    rows, block = factor.shape
    n_prow = lax.axis_size("prow")
    sections = lax.axis_size("pcol")
    piece = rows // PIECES
    f32, bf16 = jnp.float32, jnp.bfloat16
    vmem, dma = pltpu.VMEM, pltpu.SemaphoreType.DMA
    heads = sections - 1
    return pl.pallas_call(
        functools.partial(kernel, n_prow, sections),
        out_shape=jax.ShapeDtypeStruct(right_side.shape, f32),
        in_specs=[
            pl.BlockSpec(memory_space=pltpu.VMEM),
            pl.BlockSpec(memory_space=pl.ANY),
            pl.BlockSpec(memory_space=pl.ANY),
        ],
        out_specs=pl.BlockSpec(memory_space=pltpu.VMEM),
        scratch_shapes=[
            vmem((rows, block), f32), vmem((rows, block), bf16), vmem((rows, block), bf16),
            vmem((block, block), f32), vmem((block, block), bf16), vmem((block, block), bf16),
            vmem((heads, block, block), f32), vmem((heads, block, block), bf16), vmem((heads, block, block), bf16),
            vmem((block, block), bf16), vmem((block, block), bf16), vmem((rows, block), f32),
            vmem((width, block), f32), vmem((width, block), f32),
            vmem((heads, width, block), f32), vmem((2, 2, width, block), f32),
            vmem((2, 4 * width, block), bf16),
            vmem((PIECES, 2, width, piece), f32), vmem((PIECES, width, piece), f32),
            dma((2,)), dma((2, HALVES)), dma((heads, HALVES)), dma((heads, HALVES)),
            dma((PIECES,)), dma((PIECES,)),
            dma((sections, SUBS)), dma((heads, SUBS)),
            dma((sections, SUBS)), dma((sections, SUBS)), dma((heads, SUBS)),
            dma((2, 2, 2, SUBS)), dma((2, 2, SUBS)), dma((PIECES,)), dma((PIECES,)),
        ],
        compiler_params=pltpu.CompilerParams(
            collective_id=0, has_side_effects=True, vmem_limit_bytes=60 * 1024 * 1024
        ),
        name="solve_window",
    )(right_side, factor, inverses)


def solution(mesh):
    return jax.shard_map(
        per_device,
        mesh=mesh,
        in_specs=(P("pcol", "prow"), P("prow", "pcol"), P()),
        out_specs=P("pcol", "prow"),
        check_vma=False,
    )
```

```python
import functools

import jax
import jax.numpy as jnp
from jax import lax
from jax.experimental import pallas as pl
from jax.experimental.pallas import tpu as pltpu
from jax.sharding import PartitionSpec as P

MESH = pl.DeviceIdType.MESH
SUBS = 2
HALVES = 2
PIECES = 4


def split(value):
    high = value.astype(jnp.bfloat16)
    low = (value - high.astype(jnp.float32)).astype(jnp.bfloat16)
    return high, low


def dot_nt(left, right):
    return lax.dot_general(left, right, (((1,), (1,)), ((), ())), preferred_element_type=jnp.float32)


def dot_nn(left, right):
    return lax.dot_general(left, right, (((1,), (0,)), ((), ())), preferred_element_type=jnp.float32)


def contract(left, right_high, right_low):
    rows = left.shape[0]
    high, low = split(left)
    both = dot_nt(jnp.concatenate([high, low], axis=0), right_high)
    return both[:rows] + (both[rows:] + dot_nt(high, right_low))


def kernel(
    n_prow, sections, rhs, factor, inverses, out,
    fac, f_hi, f_lo, dinv, d_hi, d_lo, l_in, l_hi, l_lo, m_hi, m_lo, l_oth,
    acc, x_own, x_head, x_all, x_split, part, fin,
    local_sem, l_send, l_fwd, l_recv, swap_send, swap_recv, head_send, head_recv,
    mate_send, up_send, back_send, tree_send, x_recv, part_send, fin_recv,
):
    width = rhs.shape[0]
    block = factor.shape[1]
    piece = factor.shape[0] // PIECES
    p = lax.axis_index("prow")
    c = lax.axis_index("pcol")
    pair, parity = c // 2, c % 2
    mate = pair * 2 + 1 - parity
    over = (1 - pair) * 2 + parity
    z, x = p // 2, p % 2
    beside = z * 2 + 1 - x
    levels = n_prow // 2
    in_head = p < sections
    last = sections - 1
    folded = (pair == 0) | (p == last)
    at_once = (p >= sections) | ((p == last - 1) & (pair == 1))
    sub = width // SUBS
    half = block // HALVES

    fac_copy = pltpu.make_async_copy(factor, fac, local_sem.at[0])
    dinv_copy = pltpu.make_async_copy(
        inverses.at[pl.ds(lax.rem(p, sections) * block, block)], dinv, local_sem.at[1]
    )
    dinv_copy.start()
    fac_copy.start()

    barrier = pltpu.get_barrier_semaphore()
    above, below = lax.rem(p + 2, n_prow), lax.rem(p + n_prow - 2, n_prow)
    across = (z + 1 - 2 * (z % 2)) * 2 + 1 - x
    greeted = [(row, c) for row in (above, below, beside, across)]
    greeted += [(row, mate) for row in (above, below, beside, across)]
    greeted += [(p, lax.rem(c + step, sections)) for step in range(1, sections)]
    for device in greeted:
        pl.semaphore_signal(barrier, inc=1, device_id=device, device_id_type=MESH)
    pl.semaphore_wait(barrier, len(greeted))

    def send(src, dst, send_sem, recv_sem, row, col):
        return pltpu.make_async_remote_copy(
            src_ref=src, dst_ref=dst, send_sem=send_sem, recv_sem=recv_sem,
            device_id=(row, col), device_id_type=MESH,
        )

    def l_piece(j, h):
        return l_in.at[j, pl.ds(h * half, half)]

    def l_copy(j, h, target, way):
        return send(
            factor.at[pl.ds(h * half, half)], l_piece(j, h), l_send.at[way, h], l_recv.at[j, h], p, target
        )

    def l_forward(j, h):
        return send(l_piece(j, h), l_piece(j, h), l_fwd.at[j, h], l_recv.at[j, h], p, j ^ 3)

    def swap(m):
        rows = pl.ds(m * piece, piece)
        return send(factor.at[rows], l_oth.at[rows], swap_send.at[m], swap_recv.at[m], p, over)

    def each_piece(body):
        for m in range(PIECES):
            if m * piece < block:
                pl.when(p >= sections)(functools.partial(body, m))
            else:
                body(m)

    for j in range(sections - 1):
        @pl.when((p > j) & in_head & (c == j))
        def _():
            for h in range(HALVES):
                l_copy(j, h, j ^ 2, 0).start()
                l_copy(j, h, j ^ 1, 1).start()

    first, rest = range(PIECES // 2), range(PIECES // 2, PIECES)

    @pl.when(at_once)
    def _():
        for m in first:
            pl.when(p >= sections)(lambda: swap(m).start())
        for m in rest:
            pl.when(p < sections)(lambda: swap(m).start())

    def swap_late():
        for j in range(sections - 1):
            @pl.when((p > j) & (c == j))
            def _():
                for h in range(HALVES):
                    l_copy(j, h, j ^ 2, 0).wait_send()
        each_piece(lambda m: swap(m).start())

    dinv_copy.wait()
    d_hi[...], d_lo[...] = split(dinv[...])
    fac_copy.wait()
    pl.when((p == last) & (pair == 1))(swap_late)

    for j in range(sections - 1):
        @pl.when((p > j) & in_head & (c == j))
        def _():
            l_hi[j], l_lo[j] = split(fac[:block])

        @pl.when((p > j) & in_head & (c == (j ^ 2)))
        def _():
            for h in range(HALVES):
                l_forward(j, h).wait_recv()
                l_forward(j, h).start()
            l_hi[j], l_lo[j] = split(l_in[j])

    for j in range(sections - 1):
        @pl.when((p > j) & in_head & ((c == (j ^ 1)) | (c == (j ^ 3))))
        def _():
            for h in range(HALVES):
                l_forward(j, h).wait_recv()
            l_hi[j], l_lo[j] = split(l_in[j])

    def head_copy(s, target, col):
        rows = pl.ds(s * sub, sub)
        return send(
            x_own.at[rows], x_head.at[col, rows], head_send.at[target, s], head_recv.at[col, s], target, c
        )

    def publish_copy(ref, k, s, sems, row):
        rows = pl.ds(s * sub, sub)
        return send(
            ref.at[rows], x_all.at[k // 2, parity, rows],
            sems, x_recv.at[k // 2, parity, s], row, pair * 2 + k % 2,
        )

    def publish(ref, k, s, act):
        pl.when(parity != k % 2)(lambda: act(publish_copy(ref, k, s, mate_send.at[k, s], p)))
        pl.when((p == 2 + k % 2) & (z + 1 < levels))(
            lambda: act(publish_copy(ref, k, s, up_send.at[k, s], p + 2))
        )

    def keep(ref, k, s):
        rows = pl.ds(s * sub, sub)

        @pl.when(parity == k % 2)
        def _():
            x_all[k // 2, parity, rows] = ref[rows]

    def go_back(s, act):
        for row in range(sections - 1):
            pl.when(row < p)(lambda: act(publish_copy(x_own, p, s, back_send.at[row, s], row)))

    start = lambda copy: copy.start()
    drain = lambda copy: copy.wait_send()

    pl.when((p == last) & (pair == 0))(swap_late)

    @pl.when(in_head)
    def _():
        acc[...] = rhs[:, :block]
        for j in range(sections - 1):
            @pl.when((p == j + 1) & folded)
            def _():
                both = dot_nn(jnp.concatenate([d_hi[...], d_lo[...]], axis=0), l_hi[j])
                chain = both[:block] + (both[block:] + dot_nn(d_hi[...], l_lo[j]))
                m_hi[...], m_lo[...] = split(chain)

        for j in range(sections - 1):
            @pl.when((p > j + 1) | ((p == j + 1) & jnp.logical_not(folded)))
            def _():
                for s in range(SUBS):
                    head_copy(s, last, j).wait_recv()
                    publish(x_head.at[j], j, s, start)
                acc[...] -= contract(x_head[j], l_hi[j], l_lo[j])

        acc[...] = contract(acc[...], d_hi[...], d_lo[...])
        for s in range(SUBS):
            rows = pl.ds(s * sub, sub)
            x_own[rows] = acc[rows]
            for j in range(sections - 1):
                @pl.when((p == j + 1) & folded)
                def _():
                    head_copy(s, last, j).wait_recv()
                    x_own[rows] = acc[rows] - contract(x_head[j, rows], m_hi[...], m_lo[...])
            for target in range(1, sections):
                @pl.when((p == target - 1) | ((p < target) & (target < sections - 1)))
                def _():
                    head_copy(s, target, p).start()
            publish(x_own, p, s, start)
            for j in range(sections - 1):
                @pl.when((p == j + 1) & folded)
                def _():
                    publish(x_head.at[j], j, s, start)

        @pl.when(p < sections - 2)
        def _():
            for s in range(SUBS):
                head_copy(s, sections - 1, p).start()

        for s in range(SUBS):
            go_back(s, start)

        for s in range(SUBS):
            keep(x_own, p, s)
            for j in range(sections - 1):
                pl.when(j < p)(lambda: keep(x_head.at[j], j, s))

    @pl.when(jnp.logical_not(at_once) & (p != last))
    def _():
        swap_late()

    for m in range(PIECES):
        rows = pl.ds(m * piece, piece)
        f_hi[rows], f_lo[rows] = split(fac[rows])

    links = (
        (jnp.logical_not(in_head) & (x == parity) & (z + 1 < levels), p + 2),
        (jnp.logical_not(in_head) & (x == parity), beside),
    )

    def tree_copy(slot, side, s, way, target):
        ref = x_all.at[slot, side, pl.ds(s * sub, sub)]
        return send(ref, ref, tree_send.at[way, slot, side, s], x_recv.at[slot, side, s], target, c)

    def spread(slot):
        kept = in_head & (p >= slot * 2 + parity)
        for s in range(SUBS):
            for side in range(2):
                @pl.when(jnp.logical_not(kept & (parity == side)))
                def _():
                    tree_copy(slot, side, s, 1, beside).wait_recv()

                for way, (active, target) in enumerate(links):
                    @pl.when(active)
                    def _():
                        tree_copy(slot, side, s, way, target).start()
        high, low = split(x_all[slot].reshape(2 * width, block))
        x_split[slot, :2 * width] = high
        x_split[slot, 2 * width:] = low

    def product(slot, right_high, right_low):
        both = dot_nt(x_split[slot], right_high)
        low = dot_nt(x_split[slot, :2 * width], right_low)
        return (both[:2 * width] + (both[2 * width:] + low)).reshape(2, width, piece)

    def own(m, slot):
        rows = pl.ds(m * piece, piece)
        return product(slot, f_hi[rows], f_lo[rows])

    def other(m, slot):
        swap(m).wait_recv()
        return product(slot, *split(l_oth[pl.ds(m * piece, piece)]))

    def part_copy(m):
        return send(part.at[m, 1 - parity], fin.at[m], part_send.at[m], fin_recv.at[m], p, mate)

    def first_own(slot, m):
        part[m] = own(m, slot)

    def then_other(slot, m):
        part[m] += other(m, slot)
        part_copy(m).start()

    def whole_own(m):
        part[m] += own(m, 1)
        part_copy(m).start()

    def late_own(m):
        if m in first:
            whole_own(m)
        else:
            part[m] = own(m, 1)

    @pl.when(p >= sections)
    def _():
        for m in first:
            swap(m).wait_send()
            swap(m + PIECES // 2).start()

    leaf = jnp.logical_not(in_head) & (x != parity)
    spread(0)
    pl.when(pair == 0)(lambda: each_piece(functools.partial(first_own, 0)))

    @pl.when((pair == 1) & (p >= sections))
    def _():
        for m in first:
            part[m] = other(m, 0)

    @pl.when((pair == 1) & leaf)
    def _():
        for m in rest:
            part[m] = other(m, 0)

    spread(1)
    pl.when(pair == 0)(lambda: each_piece(functools.partial(then_other, 1)))

    @pl.when((pair == 1) & leaf)
    def _():
        each_piece(whole_own)

    @pl.when((pair == 1) & jnp.logical_not(leaf))
    def _():
        each_piece(late_own)
        for m in rest:
            then_other(0, m)

    @pl.when(in_head)
    def _():
        out[:, :block] = x_own[...]

    def finish(m):
        cols = pl.ds(m * piece, piece)
        part_copy(m).wait_recv()
        out[:, cols] = rhs[:, cols] - (part[m, parity] + fin[m])
        part_copy(m).wait_send()
        if m in rest:
            swap(m).wait_send()

    each_piece(finish)

    for j in range(sections - 1):
        @pl.when((p > j) & in_head & (c == j))
        def _():
            for h in range(HALVES):
                l_copy(j, h, j ^ 1, 1).wait_send()

        @pl.when((p > j) & in_head & (c == (j ^ 2)))
        def _():
            for h in range(HALVES):
                l_forward(j, h).wait_send()

    @pl.when(in_head)
    def _():
        for s in range(SUBS):
            for target in range(1, sections):
                @pl.when(p < target)
                def _():
                    head_copy(s, target, p).wait_send()
            publish(x_own, p, s, drain)
            go_back(s, drain)
            for j in range(sections - 1):
                pl.when(j < p)(lambda: publish(x_head.at[j], j, s, drain))

    for slot in range(2):
        for s in range(SUBS):
            for side in range(2):
                for way, (active, target) in enumerate(links):
                    @pl.when(active)
                    def _():
                        tree_copy(slot, side, s, way, target).wait_send()


def per_device(right_side, factor, inverses):
    width = right_side.shape[0]
    rows, block = factor.shape
    n_prow = lax.axis_size("prow")
    sections = lax.axis_size("pcol")
    piece = rows // PIECES
    f32, bf16 = jnp.float32, jnp.bfloat16
    vmem, dma = pltpu.VMEM, pltpu.SemaphoreType.DMA
    heads = sections - 1
    return pl.pallas_call(
        functools.partial(kernel, n_prow, sections),
        out_shape=jax.ShapeDtypeStruct(right_side.shape, f32),
        in_specs=[
            pl.BlockSpec(memory_space=pltpu.VMEM),
            pl.BlockSpec(memory_space=pl.ANY),
            pl.BlockSpec(memory_space=pl.ANY),
        ],
        out_specs=pl.BlockSpec(memory_space=pltpu.VMEM),
        scratch_shapes=[
            vmem((rows, block), f32), vmem((rows, block), bf16), vmem((rows, block), bf16),
            vmem((block, block), f32), vmem((block, block), bf16), vmem((block, block), bf16),
            vmem((heads, block, block), f32), vmem((heads, block, block), bf16), vmem((heads, block, block), bf16),
            vmem((block, block), bf16), vmem((block, block), bf16), vmem((rows, block), f32),
            vmem((width, block), f32), vmem((width, block), f32),
            vmem((heads, width, block), f32), vmem((2, 2, width, block), f32),
            vmem((2, 4 * width, block), bf16),
            vmem((PIECES, 2, width, piece), f32), vmem((PIECES, width, piece), f32),
            dma((2,)), dma((2, HALVES)), dma((heads, HALVES)), dma((heads, HALVES)),
            dma((PIECES,)), dma((PIECES,)),
            dma((sections, SUBS)), dma((heads, SUBS)),
            dma((sections, SUBS)), dma((sections, SUBS)), dma((heads, SUBS)),
            dma((2, 2, 2, SUBS)), dma((2, 2, SUBS)), dma((PIECES,)), dma((PIECES,)),
        ],
        compiler_params=pltpu.CompilerParams(
            collective_id=0, has_side_effects=True, vmem_limit_bytes=60 * 1024 * 1024
        ),
        name="solve_window",
    )(right_side, factor, inverses)


def solution(mesh):
    return jax.shard_map(
        per_device,
        mesh=mesh,
        in_specs=(P("pcol", "prow"), P("prow", "pcol"), P()),
        out_specs=P("pcol", "prow"),
        check_vma=False,
    )
```

```python
import functools

import jax
import jax.numpy as jnp
from jax import lax
from jax.experimental import pallas as pl
from jax.experimental.pallas import tpu as pltpu
from jax.sharding import PartitionSpec as P

MESH = pl.DeviceIdType.MESH
SUBS = 2
HALVES = 2
PIECES = 4


def split(value):
    high = value.astype(jnp.bfloat16)
    low = (value - high.astype(jnp.float32)).astype(jnp.bfloat16)
    return high, low


def dot_nt(left, right):
    return lax.dot_general(left, right, (((1,), (1,)), ((), ())), preferred_element_type=jnp.float32)


def dot_nn(left, right):
    return lax.dot_general(left, right, (((1,), (0,)), ((), ())), preferred_element_type=jnp.float32)


def contract(left, right_high, right_low):
    rows = left.shape[0]
    high, low = split(left)
    both = dot_nt(jnp.concatenate([high, low], axis=0), right_high)
    return both[:rows] + (both[rows:] + dot_nt(high, right_low))


def kernel(
    n_prow, sections, rhs, factor, inverses, out,
    fac, f_hi, f_lo, dinv, d_hi, d_lo, l_in, l_hi, l_lo, m_hi, m_lo, l_oth,
    acc, x_own, x_head, x_all, x_split, part, fin,
    local_sem, l_send, l_fwd, l_recv, swap_send, swap_recv, head_send, head_recv,
    mate_send, up_send, back_send, tree_send, x_recv, part_send, fin_recv,
):
    width = rhs.shape[0]
    block = factor.shape[1]
    piece = factor.shape[0] // PIECES
    p = lax.axis_index("prow")
    c = lax.axis_index("pcol")
    pair, parity = c // 2, c % 2
    mate = pair * 2 + 1 - parity
    over = (1 - pair) * 2 + parity
    z, x = p // 2, p % 2
    beside = z * 2 + 1 - x
    levels = n_prow // 2
    in_head = p < sections
    last = sections - 1
    folded = (pair == 0) | (p == last)
    at_once = (p >= sections) | ((p == last - 1) & (pair == 1))
    sub = width // SUBS
    half = block // HALVES

    fac_copy = pltpu.make_async_copy(factor, fac, local_sem.at[0])
    dinv_copy = pltpu.make_async_copy(
        inverses.at[pl.ds(lax.rem(p, sections) * block, block)], dinv, local_sem.at[1]
    )
    dinv_copy.start()
    fac_copy.start()

    barrier = pltpu.get_barrier_semaphore()
    above, below = lax.rem(p + 2, n_prow), lax.rem(p + n_prow - 2, n_prow)
    across = (z + 1 - 2 * (z % 2)) * 2 + 1 - x
    greeted = [(row, c) for row in (above, below, beside, across)]
    greeted += [(row, mate) for row in (above, below, beside, across)]
    greeted += [(p, lax.rem(c + step, sections)) for step in range(1, sections)]
    for device in greeted:
        pl.semaphore_signal(barrier, inc=1, device_id=device, device_id_type=MESH)
    pl.semaphore_wait(barrier, len(greeted))

    def send(src, dst, send_sem, recv_sem, row, col):
        return pltpu.make_async_remote_copy(
            src_ref=src, dst_ref=dst, send_sem=send_sem, recv_sem=recv_sem,
            device_id=(row, col), device_id_type=MESH,
        )

    def l_piece(j, h):
        return l_in.at[j, pl.ds(h * half, half)]

    def l_copy(j, h, target, way):
        return send(
            factor.at[pl.ds(h * half, half)], l_piece(j, h), l_send.at[way, h], l_recv.at[j, h], p, target
        )

    def l_forward(j, h):
        return send(l_piece(j, h), l_piece(j, h), l_fwd.at[j, h], l_recv.at[j, h], p, j ^ 3)

    def swap(m):
        rows = pl.ds(m * piece, piece)
        return send(factor.at[rows], l_oth.at[rows], swap_send.at[m], swap_recv.at[m], p, over)

    def each_piece(body):
        for m in range(PIECES):
            if m * piece < block:
                pl.when(p >= sections)(functools.partial(body, m))
            else:
                body(m)

    for j in range(sections - 1):
        @pl.when((p > j) & in_head & (c == j))
        def _():
            l_copy(j, 0, j ^ 2, 0).start()
            for h in range(HALVES):
                l_copy(j, h, j ^ 1, 1).start()

    first, rest = range(PIECES // 2), range(PIECES // 2, PIECES)

    @pl.when(at_once)
    def _():
        for m in first:
            pl.when(p >= sections)(lambda: swap(m).start())
        for m in rest:
            pl.when(p < sections)(lambda: swap(m).start())

    def swap_late():
        for j in range(sections - 1):
            @pl.when((p > j) & (c == j))
            def _():
                l_copy(j, HALVES - 1, j ^ 2, 0).wait_send()
        each_piece(lambda m: swap(m).start())

    dinv_copy.wait()
    d_hi[...], d_lo[...] = split(dinv[...])
    fac_copy.wait()

    for j in range(sections - 1):
        @pl.when((p > j) & in_head & (c == j))
        def _():
            l_hi[j], l_lo[j] = split(fac[:block])
            for h in range(1, HALVES):
                l_copy(j, h - 1, j ^ 2, 0).wait_send()
                l_copy(j, h, j ^ 2, 0).start()

    pl.when((p == last) & (pair == 1))(swap_late)

    for j in range(sections - 1):
        @pl.when((p > j) & in_head & folded & (c == (j ^ 2)))
        def _():
            for h in range(HALVES):
                l_forward(j, h).wait_recv()
                l_forward(j, h).start()
            l_hi[j], l_lo[j] = split(l_in[j])

    for j in range(sections - 1):
        @pl.when((p > j) & in_head & folded & ((c == (j ^ 1)) | (c == (j ^ 3))))
        def _():
            for h in range(HALVES):
                l_forward(j, h).wait_recv()
            l_hi[j], l_lo[j] = split(l_in[j])

    def head_copy(s, target, col):
        rows = pl.ds(s * sub, sub)
        return send(
            x_own.at[rows], x_head.at[col, rows], head_send.at[target, s], head_recv.at[col, s], target, c
        )

    def publish_copy(ref, k, s, sems, row):
        rows = pl.ds(s * sub, sub)
        return send(
            ref.at[rows], x_all.at[k // 2, parity, rows],
            sems, x_recv.at[k // 2, parity, s], row, pair * 2 + k % 2,
        )

    def publish(ref, k, s, act):
        pl.when(parity != k % 2)(lambda: act(publish_copy(ref, k, s, mate_send.at[k, s], p)))
        pl.when((p == 2 + k % 2) & (z + 1 < levels))(
            lambda: act(publish_copy(ref, k, s, up_send.at[k, s], p + 2))
        )

    def keep(ref, k, s):
        rows = pl.ds(s * sub, sub)

        @pl.when(parity == k % 2)
        def _():
            x_all[k // 2, parity, rows] = ref[rows]

    def go_back(s, act):
        for row in range(sections - 1):
            pl.when(row < p)(lambda: act(publish_copy(x_own, p, s, back_send.at[row, s], row)))

    start = lambda copy: copy.start()
    drain = lambda copy: copy.wait_send()

    pl.when((p == last) & (pair == 0))(swap_late)

    @pl.when(in_head)
    def _():
        acc[...] = rhs[:, :block]
        for j in range(sections - 1):
            @pl.when((p == j + 1) & folded)
            def _():
                both = dot_nn(jnp.concatenate([d_hi[...], d_lo[...]], axis=0), l_hi[j])
                chain = both[:block] + (both[block:] + dot_nn(d_hi[...], l_lo[j]))
                m_hi[...], m_lo[...] = split(chain)

        for j in range(sections - 1):
            @pl.when((p > j + 1) & folded)
            def _():
                for s in range(SUBS):
                    head_copy(s, last, j).wait_recv()
                    publish(x_head.at[j], j, s, start)
                acc[...] -= contract(x_head[j], l_hi[j], l_lo[j])

        @pl.when(jnp.logical_not(folded))
        def _():
            for h in range(HALVES):
                rows = pl.ds(h * half, half)
                for j in range(sections - 2):
                    @pl.when((p > j) & (c == (j ^ 2)))
                    def _():
                        l_forward(j, h).wait_recv()
                        l_forward(j, h).start()
                for j in range(sections - 2):
                    @pl.when((p > j) & (c == (j ^ 3)))
                    def _():
                        l_forward(j, h).wait_recv()

                    @pl.when(p > j)
                    def _():
                        if h == 0:
                            for s in range(SUBS):
                                head_copy(s, last, j).wait_recv()
                                publish(x_head.at[j], j, s, start)
                        acc[:, rows] -= contract(x_head[j], *split(l_in[j, rows]))

        acc[...] = contract(acc[...], d_hi[...], d_lo[...])
        for s in range(SUBS):
            rows = pl.ds(s * sub, sub)
            x_own[rows] = acc[rows]
            for j in range(sections - 1):
                @pl.when((p == j + 1) & folded)
                def _():
                    head_copy(s, last, j).wait_recv()
                    x_own[rows] = acc[rows] - contract(x_head[j, rows], m_hi[...], m_lo[...])
            for target in range(1, sections):
                @pl.when((p == target - 1) | ((p < target) & (target < sections - 1)))
                def _():
                    head_copy(s, target, p).start()
            publish(x_own, p, s, start)
            for j in range(sections - 1):
                @pl.when((p == j + 1) & folded)
                def _():
                    publish(x_head.at[j], j, s, start)

        @pl.when(p < sections - 2)
        def _():
            for s in range(SUBS):
                head_copy(s, sections - 1, p).start()

        for s in range(SUBS):
            go_back(s, start)

        for s in range(SUBS):
            keep(x_own, p, s)
            for j in range(sections - 1):
                pl.when(j < p)(lambda: keep(x_head.at[j], j, s))

    @pl.when(jnp.logical_not(at_once) & (p != last))
    def _():
        swap_late()

    for m in range(PIECES):
        rows = pl.ds(m * piece, piece)
        f_hi[rows], f_lo[rows] = split(fac[rows])

    links = (
        (jnp.logical_not(in_head) & (x == parity) & (z + 1 < levels), p + 2),
        (jnp.logical_not(in_head) & (x == parity), beside),
    )

    def tree_copy(slot, side, s, way, target):
        ref = x_all.at[slot, side, pl.ds(s * sub, sub)]
        return send(ref, ref, tree_send.at[way, slot, side, s], x_recv.at[slot, side, s], target, c)

    def spread(slot):
        kept = in_head & (p >= slot * 2 + parity)
        for s in range(SUBS):
            for side in range(2):
                @pl.when(jnp.logical_not(kept & (parity == side)))
                def _():
                    tree_copy(slot, side, s, 1, beside).wait_recv()

                for way, (active, target) in enumerate(links):
                    @pl.when(active)
                    def _():
                        tree_copy(slot, side, s, way, target).start()
        high, low = split(x_all[slot].reshape(2 * width, block))
        x_split[slot, :2 * width] = high
        x_split[slot, 2 * width:] = low

    def product(slot, right_high, right_low):
        both = dot_nt(x_split[slot], right_high)
        low = dot_nt(x_split[slot, :2 * width], right_low)
        return (both[:2 * width] + (both[2 * width:] + low)).reshape(2, width, piece)

    def own(m, slot):
        rows = pl.ds(m * piece, piece)
        return product(slot, f_hi[rows], f_lo[rows])

    def other(m, slot):
        swap(m).wait_recv()
        return product(slot, *split(l_oth[pl.ds(m * piece, piece)]))

    def part_copy(m):
        return send(part.at[m, 1 - parity], fin.at[m], part_send.at[m], fin_recv.at[m], p, mate)

    def first_own(slot, m):
        part[m] = own(m, slot)

    def then_other(slot, m):
        part[m] += other(m, slot)
        part_copy(m).start()

    def whole_own(m):
        part[m] += own(m, 1)
        part_copy(m).start()

    def late_own(m):
        if m in first:
            whole_own(m)
        else:
            part[m] = own(m, 1)

    @pl.when(p >= sections)
    def _():
        for m in first:
            swap(m).wait_send()
            swap(m + PIECES // 2).start()

    leaf = jnp.logical_not(in_head) & (x != parity)
    spread(0)
    pl.when(pair == 0)(lambda: each_piece(functools.partial(first_own, 0)))

    @pl.when((pair == 1) & (p >= sections))
    def _():
        for m in first:
            part[m] = other(m, 0)

    @pl.when((pair == 1) & leaf)
    def _():
        for m in rest:
            part[m] = other(m, 0)

    spread(1)
    pl.when(pair == 0)(lambda: each_piece(functools.partial(then_other, 1)))

    @pl.when((pair == 1) & leaf)
    def _():
        each_piece(whole_own)

    @pl.when((pair == 1) & jnp.logical_not(leaf))
    def _():
        each_piece(late_own)
        for m in rest:
            then_other(0, m)

    @pl.when(in_head)
    def _():
        out[:, :block] = x_own[...]

    def finish(m):
        cols = pl.ds(m * piece, piece)
        part_copy(m).wait_recv()
        out[:, cols] = rhs[:, cols] - (part[m, parity] + fin[m])
        part_copy(m).wait_send()
        if m in rest:
            swap(m).wait_send()

    each_piece(finish)

    for j in range(sections - 1):
        @pl.when((p > j) & in_head & (c == j))
        def _():
            for h in range(HALVES):
                l_copy(j, h, j ^ 1, 1).wait_send()

        @pl.when((p > j) & in_head & (c == (j ^ 2)))
        def _():
            for h in range(HALVES):
                l_forward(j, h).wait_send()

    @pl.when(in_head)
    def _():
        for s in range(SUBS):
            for target in range(1, sections):
                @pl.when(p < target)
                def _():
                    head_copy(s, target, p).wait_send()
            publish(x_own, p, s, drain)
            go_back(s, drain)
            for j in range(sections - 1):
                pl.when(j < p)(lambda: publish(x_head.at[j], j, s, drain))

    for slot in range(2):
        for s in range(SUBS):
            for side in range(2):
                for way, (active, target) in enumerate(links):
                    @pl.when(active)
                    def _():
                        tree_copy(slot, side, s, way, target).wait_send()


def per_device(right_side, factor, inverses):
    width = right_side.shape[0]
    rows, block = factor.shape
    n_prow = lax.axis_size("prow")
    sections = lax.axis_size("pcol")
    piece = rows // PIECES
    f32, bf16 = jnp.float32, jnp.bfloat16
    vmem, dma = pltpu.VMEM, pltpu.SemaphoreType.DMA
    heads = sections - 1
    return pl.pallas_call(
        functools.partial(kernel, n_prow, sections),
        out_shape=jax.ShapeDtypeStruct(right_side.shape, f32),
        in_specs=[
            pl.BlockSpec(memory_space=pltpu.VMEM),
            pl.BlockSpec(memory_space=pltpu.HBM),
            pl.BlockSpec(memory_space=pltpu.HBM),
        ],
        out_specs=pl.BlockSpec(memory_space=pltpu.VMEM),
        scratch_shapes=[
            vmem((rows, block), f32), vmem((rows, block), bf16), vmem((rows, block), bf16),
            vmem((block, block), f32), vmem((block, block), bf16), vmem((block, block), bf16),
            vmem((heads, block, block), f32), vmem((heads, block, block), bf16), vmem((heads, block, block), bf16),
            vmem((block, block), bf16), vmem((block, block), bf16), vmem((rows, block), f32),
            vmem((width, block), f32), vmem((width, block), f32),
            vmem((heads, width, block), f32), vmem((2, 2, width, block), f32),
            vmem((2, 4 * width, block), bf16),
            vmem((PIECES, 2, width, piece), f32), vmem((PIECES, width, piece), f32),
            dma((2,)), dma((2, HALVES)), dma((heads, HALVES)), dma((heads, HALVES)),
            dma((PIECES,)), dma((PIECES,)),
            dma((sections, SUBS)), dma((heads, SUBS)),
            dma((sections, SUBS)), dma((sections, SUBS)), dma((heads, SUBS)),
            dma((2, 2, 2, SUBS)), dma((2, 2, SUBS)), dma((PIECES,)), dma((PIECES,)),
        ],
        compiler_params=pltpu.CompilerParams(
            collective_id=0, has_side_effects=True, vmem_limit_bytes=40 * 1024 * 1024
        ),
        name="solve_window",
    )(right_side, factor, inverses)


def solution(mesh):
    return jax.shard_map(
        per_device,
        mesh=mesh,
        in_specs=(P("pcol", "prow"), P("prow", "pcol"), P()),
        out_specs=P("pcol", "prow"),
        check_vma=False,
    )
```

```python
import functools

import jax
import jax.numpy as jnp
from jax import lax
from jax.experimental import pallas as pl
from jax.experimental.pallas import tpu as pltpu
from jax.sharding import PartitionSpec as P

MESH = pl.DeviceIdType.MESH
SUBS = 4
HALVES = 2
PIECES = 4


def split(value):
    high = value.astype(jnp.bfloat16)
    low = (value - high.astype(jnp.float32)).astype(jnp.bfloat16)
    return high, low


def dot_nt(left, right):
    return lax.dot_general(left, right, (((1,), (1,)), ((), ())), preferred_element_type=jnp.float32)


def dot_nn(left, right):
    return lax.dot_general(left, right, (((1,), (0,)), ((), ())), preferred_element_type=jnp.float32)


def contract(left, right_high, right_low):
    rows = left.shape[0]
    high, low = split(left)
    both = dot_nt(jnp.concatenate([high, low], axis=0), right_high)
    return both[:rows] + (both[rows:] + dot_nt(high, right_low))


def kernel(
    n_prow, sections, rhs, factor, inverses, out,
    fac, f_hi, f_lo, dinv, d_hi, d_lo, l_in, l_hi, l_lo, m_hi, m_lo, l_oth,
    acc, x_own, x_head, x_all, x_split, part, fin,
    local_sem, l_send, l_fwd, l_recv, swap_send, swap_recv, head_send, head_recv,
    mate_send, up_send, back_send, tree_send, x_recv, part_send, fin_recv,
):
    width = rhs.shape[0]
    block = factor.shape[1]
    piece = factor.shape[0] // PIECES
    p = lax.axis_index("prow")
    c = lax.axis_index("pcol")
    pair, parity = c // 2, c % 2
    mate = pair * 2 + 1 - parity
    over = (1 - pair) * 2 + parity
    z, x = p // 2, p % 2
    beside = z * 2 + 1 - x
    levels = n_prow // 2
    in_head = p < sections
    last = sections - 1
    folded = (pair == 0) | (p == last)
    at_once = (p >= sections) | ((p == last - 1) & (pair == 1))
    sub = width // SUBS
    half = block // HALVES

    fac_copy = pltpu.make_async_copy(factor, fac, local_sem.at[0])
    dinv_copy = pltpu.make_async_copy(
        inverses.at[pl.ds(lax.rem(p, sections) * block, block)], dinv, local_sem.at[1]
    )
    dinv_copy.start()
    fac_copy.start()

    barrier = pltpu.get_barrier_semaphore()
    above, below = lax.rem(p + 2, n_prow), lax.rem(p + n_prow - 2, n_prow)
    across = (z + 1 - 2 * (z % 2)) * 2 + 1 - x
    greeted = [(row, c) for row in (above, below, beside, across)]
    greeted += [(row, mate) for row in (above, below, beside, across)]
    greeted += [(p, lax.rem(c + step, sections)) for step in range(1, sections)]
    for device in greeted:
        pl.semaphore_signal(barrier, inc=1, device_id=device, device_id_type=MESH)
    pl.semaphore_wait(barrier, len(greeted))

    def send(src, dst, send_sem, recv_sem, row, col):
        return pltpu.make_async_remote_copy(
            src_ref=src, dst_ref=dst, send_sem=send_sem, recv_sem=recv_sem,
            device_id=(row, col), device_id_type=MESH,
        )

    def l_piece(j, h):
        return l_in.at[j, pl.ds(h * half, half)]

    def l_copy(j, h, target, way):
        return send(
            factor.at[pl.ds(h * half, half)], l_piece(j, h), l_send.at[way, h], l_recv.at[j, h], p, target
        )

    def l_forward(j, h):
        return send(l_piece(j, h), l_piece(j, h), l_fwd.at[j, h], l_recv.at[j, h], p, j ^ 3)

    def swap(m):
        rows = pl.ds(m * piece, piece)
        return send(factor.at[rows], l_oth.at[rows], swap_send.at[m], swap_recv.at[m], p, over)

    def each_piece(body):
        for m in range(PIECES):
            if m * piece < block:
                pl.when(p >= sections)(functools.partial(body, m))
            else:
                body(m)

    for j in range(sections - 1):
        @pl.when((p > j) & in_head & (c == j))
        def _():
            for h in range(HALVES):
                l_copy(j, h, j ^ 2, 0).start()
                l_copy(j, h, j ^ 1, 1).start()

    first, rest = range(PIECES // 2), range(PIECES // 2, PIECES)

    @pl.when(at_once)
    def _():
        for m in first:
            pl.when(p >= sections)(lambda: swap(m).start())
        for m in rest:
            pl.when(p < sections)(lambda: swap(m).start())

    def swap_late():
        for j in range(sections - 1):
            @pl.when((p > j) & (c == j))
            def _():
                for h in range(HALVES):
                    l_copy(j, h, j ^ 2, 0).wait_send()
        each_piece(lambda m: swap(m).start())

    dinv_copy.wait()
    d_hi[...], d_lo[...] = split(dinv[...])
    fac_copy.wait()
    pl.when((p == last) & (pair == 1))(swap_late)

    for j in range(sections - 1):
        @pl.when((p > j) & in_head & (c == j))
        def _():
            l_hi[j], l_lo[j] = split(fac[:block])

        @pl.when((p > j) & in_head & (c == (j ^ 2)))
        def _():
            for h in range(HALVES):
                l_forward(j, h).wait_recv()
                l_forward(j, h).start()
            l_hi[j], l_lo[j] = split(l_in[j])

    for j in range(sections - 1):
        @pl.when((p > j) & in_head & ((c == (j ^ 1)) | (c == (j ^ 3))))
        def _():
            for h in range(HALVES):
                l_forward(j, h).wait_recv()
            l_hi[j], l_lo[j] = split(l_in[j])

    def head_copy(s, target, col):
        rows = pl.ds(s * sub, sub)
        return send(
            x_own.at[rows], x_head.at[col, rows], head_send.at[target, s], head_recv.at[col, s], target, c
        )

    def publish_copy(ref, k, s, sems, row):
        rows = pl.ds(s * sub, sub)
        return send(
            ref.at[rows], x_all.at[k // 2, parity, rows],
            sems, x_recv.at[k // 2, parity, s], row, pair * 2 + k % 2,
        )

    def publish(ref, k, s, act):
        pl.when(parity != k % 2)(lambda: act(publish_copy(ref, k, s, mate_send.at[k, s], p)))
        pl.when((p == 2 + k % 2) & (z + 1 < levels))(
            lambda: act(publish_copy(ref, k, s, up_send.at[k, s], p + 2))
        )

    def keep(ref, k, s):
        rows = pl.ds(s * sub, sub)

        @pl.when(parity == k % 2)
        def _():
            x_all[k // 2, parity, rows] = ref[rows]

    def go_back(s, act):
        for row in range(sections - 1):
            pl.when(row < p)(lambda: act(publish_copy(x_own, p, s, back_send.at[row, s], row)))

    start = lambda copy: copy.start()
    drain = lambda copy: copy.wait_send()

    pl.when((p == last) & (pair == 0))(swap_late)

    @pl.when(in_head)
    def _():
        acc[...] = rhs[:, :block]
        for j in range(sections - 1):
            @pl.when((p == j + 1) & folded)
            def _():
                both = dot_nn(jnp.concatenate([d_hi[...], d_lo[...]], axis=0), l_hi[j])
                chain = both[:block] + (both[block:] + dot_nn(d_hi[...], l_lo[j]))
                m_hi[...], m_lo[...] = split(chain)

        for j in range(sections - 1):
            @pl.when((p > j + 1) | ((p == j + 1) & jnp.logical_not(folded)))
            def _():
                for s in range(SUBS):
                    head_copy(s, last, j).wait_recv()
                    publish(x_head.at[j], j, s, start)
                acc[...] -= contract(x_head[j], l_hi[j], l_lo[j])

        acc[...] = contract(acc[...], d_hi[...], d_lo[...])
        for s in range(SUBS):
            rows = pl.ds(s * sub, sub)
            x_own[rows] = acc[rows]
            for j in range(sections - 1):
                @pl.when((p == j + 1) & folded)
                def _():
                    head_copy(s, last, j).wait_recv()
                    x_own[rows] = acc[rows] - contract(x_head[j, rows], m_hi[...], m_lo[...])
            for target in range(1, sections):
                @pl.when((p == target - 1) | ((p < target) & (target < sections - 1)))
                def _():
                    head_copy(s, target, p).start()
            publish(x_own, p, s, start)
            for j in range(sections - 1):
                @pl.when((p == j + 1) & folded)
                def _():
                    publish(x_head.at[j], j, s, start)

        @pl.when(p < sections - 2)
        def _():
            for s in range(SUBS):
                head_copy(s, sections - 1, p).start()

        for s in range(SUBS):
            go_back(s, start)

        for s in range(SUBS):
            keep(x_own, p, s)
            for j in range(sections - 1):
                pl.when(j < p)(lambda: keep(x_head.at[j], j, s))

    @pl.when(jnp.logical_not(at_once) & (p != last))
    def _():
        swap_late()

    for m in range(PIECES):
        rows = pl.ds(m * piece, piece)
        f_hi[rows], f_lo[rows] = split(fac[rows])

    links = (
        (jnp.logical_not(in_head) & (x == parity) & (z + 1 < levels), p + 2),
        (jnp.logical_not(in_head) & (x == parity), beside),
    )

    def tree_copy(slot, side, s, way, target):
        ref = x_all.at[slot, side, pl.ds(s * sub, sub)]
        return send(ref, ref, tree_send.at[way, slot, side, s], x_recv.at[slot, side, s], target, c)

    def spread(slot):
        kept = in_head & (p >= slot * 2 + parity)
        for s in range(SUBS):
            for side in range(2):
                @pl.when(jnp.logical_not(kept & (parity == side)))
                def _():
                    tree_copy(slot, side, s, 1, beside).wait_recv()

                for way, (active, target) in enumerate(links):
                    @pl.when(active)
                    def _():
                        tree_copy(slot, side, s, way, target).start()
        high, low = split(x_all[slot].reshape(2 * width, block))
        x_split[slot, :2 * width] = high
        x_split[slot, 2 * width:] = low

    def product(slot, right_high, right_low):
        both = dot_nt(x_split[slot], right_high)
        low = dot_nt(x_split[slot, :2 * width], right_low)
        return (both[:2 * width] + (both[2 * width:] + low)).reshape(2, width, piece)

    def own(m, slot):
        rows = pl.ds(m * piece, piece)
        return product(slot, f_hi[rows], f_lo[rows])

    def other(m, slot):
        swap(m).wait_recv()
        return product(slot, *split(l_oth[pl.ds(m * piece, piece)]))

    def part_copy(m):
        return send(part.at[m, 1 - parity], fin.at[m], part_send.at[m], fin_recv.at[m], p, mate)

    def first_own(slot, m):
        part[m] = own(m, slot)

    def then_other(slot, m):
        part[m] += other(m, slot)
        part_copy(m).start()

    def whole_own(m):
        part[m] += own(m, 1)
        part_copy(m).start()

    def late_own(m):
        if m in first:
            whole_own(m)
        else:
            part[m] = own(m, 1)

    @pl.when(p >= sections)
    def _():
        for m in first:
            swap(m).wait_send()
            swap(m + PIECES // 2).start()

    leaf = jnp.logical_not(in_head) & (x != parity)
    spread(0)
    pl.when(pair == 0)(lambda: each_piece(functools.partial(first_own, 0)))

    @pl.when((pair == 1) & (p >= sections))
    def _():
        for m in first:
            part[m] = other(m, 0)

    @pl.when((pair == 1) & leaf)
    def _():
        for m in rest:
            part[m] = other(m, 0)

    spread(1)
    pl.when(pair == 0)(lambda: each_piece(functools.partial(then_other, 1)))

    @pl.when((pair == 1) & leaf)
    def _():
        each_piece(whole_own)

    @pl.when((pair == 1) & jnp.logical_not(leaf))
    def _():
        each_piece(late_own)
        for m in rest:
            then_other(0, m)

    @pl.when(in_head)
    def _():
        out[:, :block] = x_own[...]

    def finish(m):
        cols = pl.ds(m * piece, piece)
        part_copy(m).wait_recv()
        out[:, cols] = rhs[:, cols] - (part[m, parity] + fin[m])
        part_copy(m).wait_send()
        if m in rest:
            swap(m).wait_send()

    each_piece(finish)

    for j in range(sections - 1):
        @pl.when((p > j) & in_head & (c == j))
        def _():
            for h in range(HALVES):
                l_copy(j, h, j ^ 1, 1).wait_send()

        @pl.when((p > j) & in_head & (c == (j ^ 2)))
        def _():
            for h in range(HALVES):
                l_forward(j, h).wait_send()

    @pl.when(in_head)
    def _():
        for s in range(SUBS):
            for target in range(1, sections):
                @pl.when(p < target)
                def _():
                    head_copy(s, target, p).wait_send()
            publish(x_own, p, s, drain)
            go_back(s, drain)
            for j in range(sections - 1):
                pl.when(j < p)(lambda: publish(x_head.at[j], j, s, drain))

    for slot in range(2):
        for s in range(SUBS):
            for side in range(2):
                for way, (active, target) in enumerate(links):
                    @pl.when(active)
                    def _():
                        tree_copy(slot, side, s, way, target).wait_send()


def per_device(right_side, factor, inverses):
    width = right_side.shape[0]
    rows, block = factor.shape
    n_prow = lax.axis_size("prow")
    sections = lax.axis_size("pcol")
    piece = rows // PIECES
    f32, bf16 = jnp.float32, jnp.bfloat16
    vmem, dma = pltpu.VMEM, pltpu.SemaphoreType.DMA
    heads = sections - 1
    return pl.pallas_call(
        functools.partial(kernel, n_prow, sections),
        out_shape=jax.ShapeDtypeStruct(right_side.shape, f32),
        in_specs=[
            pl.BlockSpec(memory_space=pltpu.VMEM),
            pl.BlockSpec(memory_space=pl.ANY),
            pl.BlockSpec(memory_space=pl.ANY),
        ],
        out_specs=pl.BlockSpec(memory_space=pltpu.VMEM),
        scratch_shapes=[
            vmem((rows, block), f32), vmem((rows, block), bf16), vmem((rows, block), bf16),
            vmem((block, block), f32), vmem((block, block), bf16), vmem((block, block), bf16),
            vmem((heads, block, block), f32), vmem((heads, block, block), bf16), vmem((heads, block, block), bf16),
            vmem((block, block), bf16), vmem((block, block), bf16), vmem((rows, block), f32),
            vmem((width, block), f32), vmem((width, block), f32),
            vmem((heads, width, block), f32), vmem((2, 2, width, block), f32),
            vmem((2, 4 * width, block), bf16),
            vmem((PIECES, 2, width, piece), f32), vmem((PIECES, width, piece), f32),
            dma((2,)), dma((2, HALVES)), dma((heads, HALVES)), dma((heads, HALVES)),
            dma((PIECES,)), dma((PIECES,)),
            dma((sections, SUBS)), dma((heads, SUBS)),
            dma((sections, SUBS)), dma((sections, SUBS)), dma((heads, SUBS)),
            dma((2, 2, 2, SUBS)), dma((2, 2, SUBS)), dma((PIECES,)), dma((PIECES,)),
        ],
        compiler_params=pltpu.CompilerParams(
            collective_id=0, has_side_effects=True, vmem_limit_bytes=60 * 1024 * 1024
        ),
        name="solve_window",
    )(right_side, factor, inverses)


def solution(mesh):
    return jax.shard_map(
        per_device,
        mesh=mesh,
        in_specs=(P("pcol", "prow"), P("prow", "pcol"), P()),
        out_specs=P("pcol", "prow"),
        check_vma=False,
    )
```
